32 devices in a mesh: row: 32 (over z, y, x, core), col: 1.
Axes of the slice: x: 2, y: 2, z: 4, core: 2. Of those that a mesh axis runs over, the one named last changes fastest.
Arguments:
- inputs: bfloat16 [128, 128, 256], P('row', 'col'), may hold values from -6 to 6
- preactivation: bfloat16 [128, 128, 256], P('row', 'col'), may hold values from -6 to 6
- cotangent: bfloat16 [128, 128, 256], P('row', 'col'), may hold values from -6 to 6
- spectral: bfloat16 [2, 128, 64, 5, 1024], P(None, 'row', 'col'), may hold values from -2 to 2
- bypass: bfloat16 [32, 32], replicated, may hold values from -1 to 1
Outputs:
- grad_inputs: bfloat16 [128, 128, 256], P('row', 'col')
- grad_spectral: float32 [2, 128, 64, 5, 1024], P(None, 'row', 'col')
- grad_bypass: float32 [32, 32], replicated
The draws below stay inside these ranges and needn't reach their ends.
All inputs are finite; a program needn't handle non-finite values.
Results may differ from the reference program's by a relative error of at most 0.022.
Values may be sent and summed in bfloat16 or wider, within the bound.
No kernel may reach another device: no remote copies, remote signals or barrier semaphores. Data moves between devices by JAX's collectives and lax.ppermute only.
A program may use at most 128 MiB of HBM per device.

```python
import math
import jax
import jax.numpy as jnp
from jax import lax

ROWS_DEV = 4
COLS_DEV = 128
NT = 8
C = 32
KX = 128
KY = 64
KT = 5
NX = 128
NY = 128
N_COL = 1


def block_scale(own_key, extent, shards, low, largest):
    gain = 1.0
    for axis_at, shards_of in shards:
        steps = jax.random.uniform(jax.random.fold_in(jax.random.fold_in(own_key, 6), axis_at), (shards_of,), jnp.float32, low / len(shards), largest / len(shards))
        gain = gain * jnp.repeat(jnp.exp(steps), extent[axis_at] // shards_of).reshape((-1,) + (1,) * (len(extent) - 1 - axis_at))
    return gain


def normal_values(stream_key, shape, deviation, most, pieces=(), kind=jnp.bfloat16):
    drawn = deviation * jax.random.normal(stream_key, shape, jnp.float32)
    if pieces:
        drawn = drawn * block_scale(stream_key, shape, pieces, -0.22, 0.18)
    return jnp.clip(drawn, -most, most).astype(kind)


def setup_inputs(seed: int = 0) -> dict:
    splits = jax.random.split(jax.random.key(seed), 6)
    inputs = normal_values(splits[0], (NX, NY, NT * C), 1.0, 6.0, ((0, 32),))
    preactivation = normal_values(splits[1], (NX, NY, NT * C), 1.0, 6.0, ((0, 32),))
    cotangent = normal_values(splits[2], (NX, NY, NT * C), 1.0, 6.0, ((0, 32),))
    spectral = normal_values(splits[3], (2, KX, KY, KT, C * C), (C // 4) ** -0.5, 2.0, ((1, 32),))
    bypass = normal_values(splits[4], (C, C), C ** -0.5, 1.0)
    return {"inputs": inputs, "preactivation": preactivation, "cotangent": cotangent, "spectral": spectral, "bypass": bypass}


exact_mode = lax.Precision.HIGHEST

def counting(length):
    return jnp.arange(length, dtype=jnp.int32)

def kept_freq(slot_index, keep_count):
    return jnp.where(slot_index < keep_count // 2, slot_index, slot_index - keep_count)

def phase_table(outer_index, inner_index, length, direction):
    turn_count = jnp.mod(outer_index[:, None] * inner_index[None, :], length)
    angles = turn_count.astype(jnp.float32) * (2.0 * math.pi / length)
    cosine = jnp.cos(angles)
    sine_part = direction * jnp.sin(angles)
    top_rows = jnp.stack([cosine, -sine_part], axis=1)
    low_rows = jnp.stack([sine_part, cosine], axis=1)
    return jnp.stack([top_rows, low_rows], axis=0)

def time_forward(step_count, time_modes):
    turn_count = jnp.mod(counting(step_count)[:, None] * counting(time_modes)[None, :], step_count)
    angles = turn_count.astype(jnp.float32) * (2.0 * math.pi / step_count)
    return jnp.stack([jnp.cos(angles), -jnp.sin(angles)], axis=1)

def time_inverse(step_count, time_modes):
    turn_count = jnp.mod(counting(time_modes)[:, None] * counting(step_count)[None, :], step_count)
    angles = turn_count.astype(jnp.float32) * (2.0 * math.pi / step_count)
    return jnp.stack([jnp.cos(angles), -jnp.sin(angles)], axis=0)

def gelu_slope(values):
    normal_cdf = 0.5 * (1.0 + lax.erf(values * (1.0 / math.sqrt(2.0))))
    density = jnp.exp(-0.5 * values * values) * (1.0 / math.sqrt(2.0 * math.pi))
    return normal_cdf + values * density

def mix_modes(modes_in, modes_grad, weight, factor):
    in_real = modes_in[:, 0]
    in_imag = modes_in[:, 1]
    grad_real = modes_grad[:, 0]
    grad_imag = modes_grad[:, 1]
    real_part = factor * (in_real[..., :, None] * grad_real[..., None, :] + in_imag[..., :, None] * grad_imag[..., None, :])
    imag_part = factor * (in_real[..., :, None] * grad_imag[..., None, :] - in_imag[..., :, None] * grad_real[..., None, :])
    weight_grad = jnp.stack([real_part, imag_part], axis=0)
    w_real = weight[0]
    w_imag = weight[1]
    back_real = factor * (jnp.einsum('kyscd,kysd->kysc', w_real, grad_real, precision=exact_mode) + jnp.einsum('kyscd,kysd->kysc', w_imag, grad_imag, precision=exact_mode))
    back_imag = factor * (jnp.einsum('kyscd,kysd->kysc', w_real, grad_imag, precision=exact_mode) - jnp.einsum('kyscd,kysd->kysc', w_imag, grad_real, precision=exact_mode))
    return (weight_grad, jnp.stack([back_real, back_imag], axis=1))

def reference(inputs, preactivation, cotangent, spectral, bypass):
    factor = 1.0 / math.sqrt(float(NX * NY * NT * KX * KY * KT))
    forward_t = time_forward(NT, KT)
    inverse_t = time_inverse(NT, KT)
    col_table = phase_table(counting(KY), counting(NY), NY, -1.0).reshape(2, KY, 2, N_COL, COLS_DEV)
    inverse_cols = phase_table(counting(NY), counting(KY), NY, 1.0)
    row_freqs = kept_freq(counting(KX), KX)
    block_count = NX // ROWS_DEV

    def block_grad(first_row):
        pre_block = lax.dynamic_slice_in_dim(preactivation, first_row, ROWS_DEV, 0)
        cot_block = lax.dynamic_slice_in_dim(cotangent, first_row, ROWS_DEV, 0)
        slopes = gelu_slope(pre_block.astype(jnp.float32))
        return (cot_block.astype(jnp.float32) * slopes).astype(jnp.bfloat16)

    def to_cols(field):
        cube_view = field.astype(jnp.float32).reshape(ROWS_DEV, N_COL, COLS_DEV, NT, C)
        in_time = jnp.einsum('rjytc,tqs->rjyqsc', cube_view, forward_t, precision=exact_mode)
        partial_sums = jnp.einsum('akpjy,rjypsc->jraksc', col_table, in_time, precision=exact_mode)
        rounded = lax.optimization_barrier(partial_sums.astype(jnp.bfloat16))
        return lax.optimization_barrier(jnp.sum(rounded.astype(jnp.float32), axis=0))

    def forward_step(running, block_index):
        modes_in, modes_grad, bypass_acc = running
        first_row = (block_index * ROWS_DEV).astype(jnp.int32)
        block_in = lax.dynamic_slice_in_dim(inputs, first_row, ROWS_DEV, 0)
        pre_grad = block_grad(first_row)
        bypass_acc = bypass_acc + jnp.einsum('nc,nd->cd', block_in.reshape(-1, C), pre_grad.reshape(-1, C), preferred_element_type=jnp.float32)
        phases = phase_table(row_freqs, first_row + counting(ROWS_DEV), NX, -1.0)
        modes_in = modes_in + jnp.einsum('akpr,rpysc->kaysc', phases, to_cols(block_in), precision=exact_mode)
        modes_grad = modes_grad + jnp.einsum('akpr,rpysc->kaysc', phases, to_cols(pre_grad), precision=exact_mode)
        return ((modes_in, modes_grad, bypass_acc), None)
    start_state = (jnp.zeros((KX, 2, KY, KT, C), jnp.float32), jnp.zeros((KX, 2, KY, KT, C), jnp.float32), jnp.zeros((C, C), jnp.float32))
    final_state, unused_out = lax.scan(forward_step, start_state, counting(block_count))
    modes_in, modes_grad, bypass_acc = final_state
    weight = spectral.astype(jnp.float32).reshape(2, KX, KY, KT, C, C)
    weight_grad, back_modes = mix_modes(modes_in, modes_grad, weight, factor)
    grad_spectral = weight_grad.reshape(2, KX, KY, KT, C * C)
    grad_bypass = bypass_acc * (1.0 / math.sqrt(float(NX * NY * NT)))

    def backward_block(block_index):
        first_row = (block_index * ROWS_DEV).astype(jnp.int32)
        phases = phase_table(first_row + counting(ROWS_DEV), row_freqs, NX, 1.0)
        rows_back = jnp.einsum('axpk,kpysc->xaysc', phases, back_modes, precision=exact_mode)
        cells_y = jnp.einsum('aypk,rpksc->ryasc', inverse_cols, rows_back, precision=exact_mode)
        kernel_grad = jnp.einsum('ryasc,ast->rytc', cells_y, inverse_t, precision=exact_mode)
        pre_grad = block_grad(first_row)
        bypass_grad = jnp.einsum('nd,cd->nc', pre_grad.reshape(-1, C), bypass, preferred_element_type=jnp.float32)
        total_grad = kernel_grad.reshape(-1, C) + bypass_grad
        return total_grad.reshape(ROWS_DEV, NY, NT * C).astype(jnp.bfloat16)
    grad_inputs = lax.map(backward_block, counting(block_count)).reshape(NX, NY, NT * C)
    return (grad_inputs, grad_spectral, grad_bypass)
```

```python
import math

import jax
import jax.numpy as jnp
import numpy as np
from jax import lax
from jax.experimental import pallas as pl
from jax.experimental.pallas import tpu as pltpu
from jax.sharding import PartitionSpec as P

exact_mode = lax.Precision.HIGHEST


def counting(length):
    return jnp.arange(length, dtype=jnp.int32)


def kept_freq(slot_index, keep_count):
    return jnp.where(slot_index < keep_count // 2, slot_index, slot_index - keep_count)


def phase_table(outer_index, inner_index, length, direction):
    turn_count = jnp.mod(outer_index[:, None] * inner_index[None, :], length)
    angles = turn_count.astype(jnp.float32) * (2.0 * math.pi / length)
    cosine = jnp.cos(angles)
    sine_part = direction * jnp.sin(angles)
    top_rows = jnp.stack([cosine, -sine_part], axis=1)
    low_rows = jnp.stack([sine_part, cosine], axis=1)
    return jnp.stack([top_rows, low_rows], axis=0)


def time_forward(step_count, time_modes):
    turn_count = jnp.mod(counting(step_count)[:, None] * counting(time_modes)[None, :], step_count)
    angles = turn_count.astype(jnp.float32) * (2.0 * math.pi / step_count)
    return jnp.stack([jnp.cos(angles), -jnp.sin(angles)], axis=1)


def time_inverse(step_count, time_modes):
    turn_count = jnp.mod(counting(time_modes)[:, None] * counting(step_count)[None, :], step_count)
    angles = turn_count.astype(jnp.float32) * (2.0 * math.pi / step_count)
    return jnp.stack([jnp.cos(angles), -jnp.sin(angles)], axis=0)


def gelu_slope(values):
    normal_cdf = 0.5 * (1.0 + lax.erf(values * (1.0 / math.sqrt(2.0))))
    density = jnp.exp(-0.5 * values * values) * (1.0 / math.sqrt(2.0 * math.pi))
    return normal_cdf + values * density


def mix_modes(modes_in, modes_grad, weight, factor):
    in_real = modes_in[:, 0]
    in_imag = modes_in[:, 1]
    grad_real = modes_grad[:, 0]
    grad_imag = modes_grad[:, 1]
    real_part = factor * (
        in_real[..., :, None] * grad_real[..., None, :]
        + in_imag[..., :, None] * grad_imag[..., None, :]
    )
    imag_part = factor * (
        in_real[..., :, None] * grad_imag[..., None, :]
        - in_imag[..., :, None] * grad_real[..., None, :]
    )
    weight_grad = jnp.stack([real_part, imag_part], axis=0)
    w_real = weight[0]
    w_imag = weight[1]
    back_real = factor * (
        jnp.einsum("kyscd,kysd->kysc", w_real, grad_real, precision=exact_mode)
        + jnp.einsum("kyscd,kysd->kysc", w_imag, grad_imag, precision=exact_mode)
    )
    back_imag = factor * (
        jnp.einsum("kyscd,kysd->kysc", w_real, grad_imag, precision=exact_mode)
        - jnp.einsum("kyscd,kysd->kysc", w_imag, grad_real, precision=exact_mode)
    )
    return (weight_grad, jnp.stack([back_real, back_imag], axis=1))


def general_local(inputs, preactivation, cotangent, spectral, bypass):
    row_count, col_count, packed = inputs.shape
    chan_count = bypass.shape[0]
    step_count = packed // chan_count
    time_modes = spectral.shape[3]
    owned_row_modes = spectral.shape[1]
    owned_col_modes = spectral.shape[2]
    row_parts = lax.axis_size("row")
    col_parts = lax.axis_size("col")
    row_modes = owned_row_modes * row_parts
    col_modes = owned_col_modes * col_parts
    total_x = row_count * row_parts
    total_y = col_count * col_parts
    factor = 1.0 / math.sqrt(
        float(total_x * total_y * step_count * row_modes * col_modes * time_modes)
    )
    row_start = lax.axis_index("row") * row_count
    col_start = lax.axis_index("col") * col_count
    mode_width = owned_col_modes * time_modes * chan_count
    slopes = gelu_slope(preactivation.astype(jnp.float32))
    pre_grad = (cotangent.astype(jnp.float32) * slopes).astype(jnp.bfloat16)
    flat_inputs = inputs.reshape(-1, chan_count)
    flat_grad = pre_grad.reshape(-1, chan_count)
    local_bypass = jnp.einsum(
        "nc,nd->cd", flat_inputs, flat_grad, preferred_element_type=jnp.float32
    )
    bypass_total = lax.psum(local_bypass, ("row", "col"))
    grad_bypass = bypass_total * (1.0 / math.sqrt(float(total_x * total_y * step_count)))
    forward_t = time_forward(step_count, time_modes)
    col_table = phase_table(counting(col_modes), col_start + counting(col_count), total_y, -1.0)

    def column_terms(field):
        cube_view = field.astype(jnp.float32).reshape(row_count, col_count, step_count, chan_count)
        in_time = jnp.einsum("rytc,tqs->ryqsc", cube_view, forward_t, precision=exact_mode)
        return jnp.einsum("akpy,rypsc->raksc", col_table, in_time, precision=exact_mode)

    col_in, col_grad = (
        lax.psum_scatter(
            column_terms(inputs).astype(jnp.bfloat16), "col", scatter_dimension=2, tiled=True
        ).astype(jnp.float32),
        lax.psum_scatter(
            column_terms(pre_grad).astype(jnp.bfloat16), "col", scatter_dimension=2, tiled=True
        ).astype(jnp.float32),
    )
    flat_in = col_in.reshape(row_count, 2, mode_width)
    flat_cols = col_grad.reshape(row_count, 2, mode_width)
    stacked = jnp.stack([flat_in, flat_cols], axis=2)
    frequencies = kept_freq(counting(owned_row_modes * lax.axis_size("row")), row_modes)
    phases = phase_table(frequencies, row_start + counting(row_count), total_x, -1.0)
    owned_modes = lax.psum_scatter(
        jnp.einsum("akpr,rpbm->kabm", phases, stacked, precision=exact_mode),
        "row",
        scatter_dimension=0,
        tiled=True,
    )
    modes_in = owned_modes[:, :, 0]
    modes_grad = owned_modes[:, :, 1]
    mode_shape = (owned_row_modes, 2, owned_col_modes, time_modes, chan_count)
    weight = spectral.astype(jnp.float32).reshape(
        2, owned_row_modes, owned_col_modes, time_modes, chan_count, chan_count
    )
    weight_grad, back_modes = mix_modes(
        modes_in.reshape(mode_shape), modes_grad.reshape(mode_shape), weight, factor
    )
    grad_spectral = weight_grad.reshape(spectral.shape)
    flat_back = back_modes.reshape(owned_row_modes, 2, mode_width)
    mode_piece = lax.all_gather(flat_back, "row", axis=0, tiled=True)
    span_count = mode_piece.shape[0]
    frequencies = kept_freq(counting(span_count), row_modes)
    phases = phase_table(row_start + counting(row_count), frequencies, total_x, 1.0)
    rows_back = jnp.einsum("axpk,kpm->xam", phases, mode_piece, precision=exact_mode)
    rows_view = rows_back.reshape(row_count, 2, owned_col_modes, time_modes, chan_count)
    col_piece = lax.all_gather(rows_view.astype(jnp.bfloat16), "col", axis=2, tiled=True).astype(
        jnp.float32
    )
    span_count = col_piece.shape[2]
    phases = phase_table(col_start + counting(col_count), counting(span_count), total_y, 1.0)
    cells_y = jnp.zeros(
        (row_count, col_count, 2, time_modes, chan_count), jnp.float32
    ) + jnp.einsum("aypk,rpksc->ryasc", phases, col_piece, precision=exact_mode)
    kernel_grad = jnp.einsum(
        "ryasc,ast->rytc", cells_y, time_inverse(step_count, time_modes), precision=exact_mode
    )
    bypass_grad = jnp.einsum("nd,cd->nc", flat_grad, bypass, preferred_element_type=jnp.float32)
    total_grad = kernel_grad.reshape(-1, chan_count) + bypass_grad
    grad_inputs = total_grad.reshape(inputs.shape).astype(jnp.bfloat16)
    return (grad_inputs, grad_spectral, grad_bypass)


BF = jnp.bfloat16
LANES = 128
SUB = 8


def dot(a, b):
    return jnp.dot(a, b, preferred_element_type=jnp.float32)


def cos_sin(turns, length):
    angles = 2.0 * np.pi * np.mod(turns, length) / length
    return np.cos(angles), np.sin(angles)


def build_tables(parts, rows, cols, steps, chans, row_modes, pair, kept, col_modes, time_modes):
    lead = LANES // chans
    eye = np.eye(chans)
    t_index = np.arange(steps)
    tables = {}
    cos_t, sin_t = cos_sin(np.outer(t_index, np.arange(time_modes)), steps)
    base = np.concatenate([np.kron(cos_t[:, :lead], eye), np.kron(-sin_t[:, :lead], eye)], axis=1)
    last = np.kron(cos_t[:, lead:], eye)
    blank = np.zeros_like(last)
    tables["time_base"] = base
    tables["time_last_in"] = np.concatenate(
        [last, blank, blank, blank, blank, -last, blank, blank], axis=1
    )
    tables["time_last_grad"] = np.concatenate(
        [blank, blank, last, blank, blank, blank, blank, -last], axis=1
    )
    ky = np.arange(col_modes)
    y = np.arange(cols)
    cos_y, sin_y = cos_sin(np.outer(ky, y), cols)
    same_row = np.eye(rows)
    tables["col_cos"] = np.einsum("ky,rs->krsy", cos_y, same_row).reshape(col_modes * rows, rows * cols)
    tables["col_sin"] = np.einsum("ky,rs->krsy", sin_y, same_row).reshape(col_modes * rows, rows * cols)
    slot = np.arange(row_modes)
    freq = np.where(slot < row_modes // 2, slot, slot - row_modes)
    total_x = parts * rows
    cos_x, sin_x = cos_sin(np.outer(freq, np.arange(total_x)), total_x)
    same_pair = np.eye(pair)

    def spread(matrix):
        blocks = matrix.reshape(parts, kept, parts, rows)
        return np.einsum("ekdr,pq->epkdqr", blocks, same_pair).reshape(
            parts * pair * kept, parts * pair * rows
        )

    tables["row_cos"] = spread(cos_x)
    tables["row_sin"] = spread(sin_x)
    tables["back_cos"] = spread(cos_x).T
    tables["back_sin"] = spread(sin_x).T
    swap = np.kron(np.array([[0.0, -1.0], [1.0, 0.0]]), eye)
    tables["swap"] = np.kron(np.eye(LANES // (2 * chans)), swap)
    order = np.zeros((kept, col_modes, parts, pair, kept))
    for k in range(kept):
        for e in range(parts):
            for p in range(pair):
                order[k, e * pair + p, e, p, k] = 1.0
    tables["order"] = order.reshape(kept * col_modes, parts * pair * kept)
    tables["unorder"] = tables["order"].T
    wide = chans * chans
    repeat = np.kron(eye, np.ones((1, chans)))
    tiled = np.kron(np.ones((1, lead)), eye)
    group = np.zeros((lead + 1, LANES, wide))
    for k in range(lead):
        group[k, k * chans : (k + 1) * chans] = repeat
    extra = np.zeros((LANES, wide))
    extra[chans : 2 * chans] = repeat
    group[lead, :chans] = repeat
    tables["repeat"] = np.concatenate([group, extra[None]], axis=0)
    tiles = np.zeros((lead + 2, LANES, LANES))
    for k in range(lead):
        tiles[k, k * chans : (k + 1) * chans] = tiled
    tiles[lead, 2 * chans : 3 * chans] = tiled
    tiles[lead + 1, 3 * chans : 4 * chans] = tiled
    tables["tile"] = tiles
    tables["sums"] = np.tile(repeat.T, (1, lead))
    re_c, re_s = np.kron(cos_t.T, eye), np.kron(sin_t.T, eye)
    cut = lead * chans
    rest = np.zeros((LANES - 2 * chans, steps * chans))
    to_cos = np.concatenate([re_c[:cut], -re_s[:cut], re_c[cut:], -re_s[cut:], rest], axis=0)
    to_sin = np.concatenate([-re_s[:cut], -re_c[:cut], -re_s[cut:], -re_c[cut:], rest], axis=0)
    tables["time_back"] = np.concatenate([to_cos, to_sin], axis=1)
    tables["col_back"] = np.concatenate([tables["col_cos"].T, tables["col_sin"].T], axis=1)
    place = np.zeros((parts, SUB, chans))
    for c in range(chans):
        place[c, :, c] = 1.0
    tables["place"] = place.reshape(parts * SUB, chans)
    pick = np.zeros((parts, SUB))
    pick[:, 0] = 1.0
    tables["total"] = np.broadcast_to(pick.reshape(1, -1), (parts * SUB, parts * SUB))
    first = np.zeros((chans, parts, SUB))
    for c in range(chans):
        first[c, c, 0] = 1.0
    tables["first"] = first.reshape(chans, parts * SUB)
    tables["spread_chan"] = np.kron(np.ones((steps, 1)), eye)
    return {name: np.asarray(table, np.float32).astype(jnp.bfloat16) for name, table in tables.items()}


def call(kernel, out_shapes, *operands, scratch=(), far=(), limit=12, keep=True):
    near = pl.BlockSpec(memory_space=pltpu.VMEM)
    stay = pl.BlockSpec(memory_space=pltpu.HBM)
    space = lambda i: pltpu.HBM if i in far else pltpu.VMEM
    operands = [pltpu.with_memory_space_constraint(a, space(i)) for i, a in enumerate(operands)]
    hold = lambda a: pltpu.VMEM(a.shape, a.dtype) if keep else a
    return pl.pallas_call(
        kernel,
        out_shape=jax.tree.map(hold, out_shapes),
        in_specs=[stay if i in far else near for i in range(len(operands))],
        out_specs=jax.tree.map(lambda _: near, out_shapes),
        scratch_shapes=list(scratch),
        compiler_params=pltpu.CompilerParams(vmem_limit_bytes=limit * 1024 * 1024),
    )(*operands)


def lane_blocks(values):
    return [values[:, i * LANES : (i + 1) * LANES] for i in range(values.shape[1] // LANES)]


def pack(blocks):
    parts = blocks[0].shape[0] // SUB
    stacked = jnp.concatenate([b.reshape(parts, SUB, LANES) for b in blocks], axis=1)
    return stacked.reshape(-1, LANES).astype(BF)


def unpack(rows, count):
    cube = rows.astype(jnp.float32).reshape(-1, count * SUB, LANES)
    return [cube[:, i * SUB : (i + 1) * SUB].reshape(-1, LANES).astype(BF) for i in range(count)]


def lane_group(shape, chans):
    return lax.broadcasted_iota(jnp.int32, shape, 1) // chans


def halves(values, chans):
    high = values.astype(BF).astype(jnp.float32)
    group = lane_group(values.shape, chans)
    return jnp.where(group == 2, high, jnp.where(group == 3, values - high, 0.0))


def diagonal(values, chans):
    row_step = lax.broadcasted_iota(jnp.int32, values.shape, 0) // chans
    return jnp.where(row_step == lane_group(values.shape, chans), values, 0.0)


def start_copies(sems, *pairs):
    copies = [pltpu.make_async_copy(src, dst, sems.at[i]) for i, (src, dst) in enumerate(pairs)]
    for copy in copies:
        copy.start()
    return copies


def columns_kernel(
    in_hbm, pre_hbm, cot_hbm, time_hbm, col_hbm, square_hbm, swap_hbm, tile_hbm, sums_hbm,
    out_ref, grad_ref, square_ref, swap_ref, tile_ref, sums_ref,
    in_ref, pre_ref, cot_ref, time_ref, col_ref, sems,
):
    copies = start_copies(
        sems,
        (pre_hbm, pre_ref), (cot_hbm, cot_ref), (in_hbm, in_ref), (time_hbm, time_ref), (col_hbm, col_ref),
        (square_hbm, square_ref), (swap_hbm, swap_ref), (tile_hbm, tile_ref), (sums_hbm, sums_ref),
    )
    rows, cols, width = in_ref.shape
    copies[0].wait()
    slopes = gelu_slope(pre_ref[...].reshape(rows * cols, width).astype(jnp.float32))
    copies[1].wait()
    grad = (cot_ref[...].reshape(rows * cols, width).astype(jnp.float32) * slopes).astype(BF)
    grad_ref[...] = grad
    copies[2].wait()
    copies[3].wait()
    field = in_ref[...].reshape(rows * cols, width)
    base, last_in, last_grad = [time_ref[i * width : (i + 1) * width] for i in range(3)]
    time_in = dot(field, base)
    time_grad = dot(grad, base)
    last = dot(field, last_in) + dot(grad, last_grad)
    in_re, in_im = time_in[:, :LANES], time_in[:, LANES:]
    gr_re, gr_im = time_grad[:, :LANES], time_grad[:, LANES:]
    direct = jnp.concatenate([in_re, in_im, gr_re, gr_im, last[:, :LANES]], axis=1).astype(BF)
    turned = jnp.concatenate([in_im, -in_re, gr_im, -gr_re, last[:, LANES:]], axis=1).astype(BF)
    copies[4].wait()
    half = col_ref.shape[0] // 2
    modes = dot(col_ref[:half], direct) + dot(col_ref[half:], turned)
    out_ref[...] = pack(lane_blocks(modes))
    for copy in copies[5:]:
        copy.wait()


def bypass_terms(field, grad, place, chans):
    products = lax.dot_general(
        field, grad, (((0,), (0,)), ((), ())), preferred_element_type=jnp.float32
    )
    products = diagonal(products, chans)
    partial = products[:chans]
    for step in range(1, field.shape[1] // chans):
        partial = partial + products[step * chans : (step + 1) * chans]
    folded = sum(lane_blocks(partial))
    shift = LANES // 2
    while shift >= chans:
        folded = folded + pltpu.roll(folded, shift, 1)
        shift //= 2
    return dot(place, halves(folded, chans).astype(BF))


def mixing_kernel(sent_hbm, grad_hbm, long_hbm, bypass_ref, spread_ref, mixed_ref, long_ref, grad_ref, sems):
    del sent_hbm
    copies = start_copies(sems, (grad_hbm, grad_ref), (long_hbm, long_ref))
    chans = bypass_ref.shape[0]
    spread = spread_ref[...]
    across = lax.dot_general(
        bypass_ref[...], spread, (((0,), (1,)), ((), ())), preferred_element_type=jnp.float32
    ).astype(BF)
    matrix = diagonal(dot(spread, across), chans).astype(BF)
    copies[0].wait()
    mixed_ref[...] = dot(grad_ref[...], matrix)
    copies[1].wait()


def rows_kernel(in_ref, square_ref, swap_ref, out_ref):
    in_re, in_im, gr_re, gr_im, last = unpack(in_ref[...], 5)
    size = square_ref.shape[1]
    turned_last = dot(last, swap_ref[...]).astype(BF)
    direct = jnp.concatenate([in_re, in_im, gr_re, gr_im, last], axis=1)
    turned = jnp.concatenate([in_im, -in_re, gr_im, -gr_re, turned_last], axis=1)
    modes = dot(square_ref[:size], direct) + dot(square_ref[size : 2 * size], turned)
    out_ref[...] = pack(lane_blocks(modes))


def back_kernel(
    in_ref, grad_ref, weight_ref, field_ref, square_ref, tile_ref, sums_ref, place_ref, out_ref, modes_ref,
    *, factor,
):
    chans = place_ref.shape[1]
    size = square_ref.shape[1]
    lanes = jnp.concatenate(unpack(in_ref[...], 5), axis=1)
    modes = dot(square_ref[4 * size : 5 * size], lanes).astype(BF)
    modes_ref[...] = modes
    rows, cols, width = field_ref.shape
    terms = bypass_terms(field_ref[...].reshape(rows * cols, width), grad_ref[...], place_ref[...], chans)
    steps = weight_ref.shape[2]
    wide = weight_ref.shape[4]
    lead = LANES // chans
    gr_re, gr_im, last = lane_blocks(modes)[2:]
    first = jnp.concatenate([gr_re, gr_im], axis=0)
    group = lane_group((size, LANES), chans)
    re_sum = im_sum = jnp.zeros((size, LANES), jnp.float32)
    for k in range(steps):
        if k < lead:
            g_both = dot(first, tile_ref[k]).astype(BF)
            g_re, g_im = g_both[:size], g_both[size:]
        else:
            g_re, g_im = dot(last, tile_ref[lead]).astype(BF), dot(last, tile_ref[lead + 1]).astype(BF)
        p_re, p_im = [], []
        for j in range(wide // LANES):
            w_re = weight_ref[0, :, k, :, j * LANES : (j + 1) * LANES].reshape(size, LANES)
            w_im = weight_ref[1, :, k, :, j * LANES : (j + 1) * LANES].reshape(size, LANES)
            p_re.append(w_re * g_re + w_im * g_im)
            p_im.append(w_re * g_im - w_im * g_re)
        both = jnp.concatenate([jnp.concatenate(p_re, axis=1), jnp.concatenate(p_im, axis=1)], axis=0)
        summed = dot(both, sums_ref[...])
        if k < lead:
            re_sum = jnp.where(group == k, summed[:size], re_sum)
            im_sum = jnp.where(group == k, summed[size:], im_sum)
        else:
            last_sum = jnp.where(group == 0, summed[:size], jnp.where(group == 1, summed[size:], 0.0))
    back = (jnp.concatenate([re_sum, im_sum, last_sum], axis=1) * factor).astype(BF)
    re, im, last = lane_blocks(dot(square_ref[5 * size : 6 * size], back))
    out_ref[...] = pack([re, im, last + terms])


def weight_kernel(modes_ref, repeat_ref, tile_ref, out_ref, *, factor):
    modes = modes_ref[...]
    in_re, in_im, gr_re, gr_im, last = [modes[:, i * LANES : (i + 1) * LANES] for i in range(5)]
    steps = out_ref.shape[2]
    lead = tile_ref.shape[0] - 2
    wide = out_ref.shape[-1]
    for k in range(steps):
        if k < lead:
            a_re, a_im = dot(in_re, repeat_ref[k]), dot(in_im, repeat_ref[k])
            b_re, b_im = dot(gr_re, tile_ref[k]), dot(gr_im, tile_ref[k])
        else:
            a_re, a_im = dot(last, repeat_ref[lead]), dot(last, repeat_ref[lead + 1])
            b_re, b_im = dot(last, tile_ref[lead]), dot(last, tile_ref[lead + 1])
        b_re = jnp.concatenate([b_re * factor] * (wide // LANES), axis=1)
        b_im = jnp.concatenate([b_im * factor] * (wide // LANES), axis=1)
        out_ref[0, 0, k] = a_re * b_re + a_im * b_im
        out_ref[1, 0, k] = a_re * b_im - a_im * b_re


def rows_back_kernel(in_ref, square_ref, swap_ref, out_ref, *, chans):
    re, im, tail = unpack(in_ref[...], 3)
    size = square_ref.shape[1]
    group = lane_group(tail.shape, chans)
    last = jnp.where(group < 2, tail.astype(jnp.float32), 0.0).astype(BF)
    turned_last = dot(-last, swap_ref[...]).astype(BF)
    direct = jnp.concatenate([re, im, last], axis=1)
    turned = jnp.concatenate([-im, re, turned_last], axis=1)
    rows = dot(square_ref[2 * size : 3 * size], direct) + dot(square_ref[3 * size : 4 * size], turned)
    summed = dot(square_ref[6 * size : 7 * size], tail)
    summed = summed + pltpu.roll(summed, LANES - chans, 1)
    summed = jnp.where(group == 2, summed, 0.0)
    summed = summed + pltpu.roll(summed, chans, 1)
    re, im, last = lane_blocks(rows)
    out_ref[...] = pack([re, im, last + halves(summed, chans)])


def columns_back_kernel(in_ref, mixed_ref, square_ref, long_ref, out_ref, bypass_ref, *, factor):
    rows, cols, width = out_ref.shape
    chans = bypass_ref.shape[0]
    size = square_ref.shape[1]
    blocks = unpack(in_ref[...], 3)
    lanes = jnp.concatenate(blocks, axis=1)
    height = lanes.shape[1]
    steps = dot(lanes, long_ref[:height]).astype(BF)
    stacked = jnp.concatenate([steps[:, :width], steps[:, width:]], axis=0)
    total = dot(long_ref[height:], stacked) + mixed_ref[...]
    out_ref[...] = total.reshape(rows, cols, width).astype(BF)
    sums = dot(square_ref[7 * size :], blocks[2])
    sums = pltpu.roll(sums + pltpu.roll(sums, LANES - chans, 1), LANES // 2, 1)
    bypass_ref[...] = sums[:, :chans] * factor


def local(inputs, preactivation, cotangent, spectral, bypass):
    rows, cols, width = inputs.shape
    chans = bypass.shape[0]
    steps = width // chans
    kept, col_modes, time_modes, wide = spectral.shape[1:]
    parts = lax.axis_size("row")
    pair = col_modes // parts
    fits = (
        lax.axis_size("col") == 1
        and col_modes % parts == 0
        and pair * rows == SUB
        and pair * kept == SUB
        and parts == chans
        and 4 * chans == LANES
        and time_modes == 5
        and steps == 8
        and cols % LANES == 0
    )
    if not fits:
        return general_local(inputs, preactivation, cotangent, spectral, bypass)
    row_modes = kept * parts
    total_x = rows * parts
    factor = 1.0 / math.sqrt(float(total_x * cols * steps * row_modes * col_modes * time_modes))
    bypass_factor = 1.0 / math.sqrt(float(total_x * cols * steps))
    tables = build_tables(parts, rows, cols, steps, chans, row_modes, pair, kept, col_modes, time_modes)
    stack = lambda *names: jnp.asarray(np.concatenate([tables[name] for name in names], axis=0))
    time_table = stack("time_base", "time_last_in", "time_last_grad")
    col_table = stack("col_cos", "col_sin")
    square = stack("row_cos", "row_sin", "back_cos", "back_sin", "order", "unorder", "total", "first")
    long = stack("time_back", "col_back")
    swap, tile, repeat, sums, spread, place = [
        jnp.asarray(tables[name]) for name in ("swap", "tile", "repeat", "sums", "spread_chan", "place")
    ]

    def swap_parts(array):
        return lax.all_to_all(array, "row", 0, 0, tiled=True)

    like = lambda array: jax.ShapeDtypeStruct(array.shape, array.dtype)
    shape = jax.ShapeDtypeStruct
    chunk = parts * SUB
    field = (rows * cols, width)
    sent, pre_grad, square, swap, tile, sums = call(
        columns_kernel,
        (shape((5 * chunk, LANES), BF), shape(field, BF)) + tuple(like(a) for a in (square, swap, tile, sums)),
        inputs, preactivation, cotangent, time_table, col_table, square, swap, tile, sums,
        far=range(9),
        scratch=[pltpu.VMEM(a.shape, a.dtype) for a in (inputs, inputs, inputs, time_table, col_table)]
        + [pltpu.SemaphoreType.DMA((9,))],
    )
    sent = call(rows_kernel, shape((5 * chunk, LANES), BF), swap_parts(sent), square, swap)
    weight = spectral.transpose(0, 1, 3, 2, 4)
    sent, modes = call(
        lambda *refs: back_kernel(*refs, factor=factor),
        (shape((3 * chunk, LANES), BF), shape((kept * col_modes, 5 * LANES), BF)),
        swap_parts(sent), pre_grad, weight, inputs, square, tile, sums, place,
    )
    whole = lambda a: pl.BlockSpec(a.shape, lambda i: (0,) * a.ndim)
    grad_spectral = pl.pallas_call(
        lambda *refs: weight_kernel(*refs, factor=factor),
        grid=(kept,),
        out_shape=shape((2, kept, time_modes, col_modes, wide), jnp.float32),
        in_specs=[pl.BlockSpec((col_modes, 5 * LANES), lambda i: (i, 0)), whole(repeat), whole(tile)],
        out_specs=pl.BlockSpec((2, 1, time_modes, col_modes, wide), lambda i: (0, i, 0, 0, 0)),
        compiler_params=pltpu.CompilerParams(vmem_limit_bytes=16 * 1024 * 1024),
    )(modes, repeat, tile).transpose(0, 1, 3, 2, 4)
    sent = call(
        lambda *refs: rows_back_kernel(*refs, chans=chans),
        shape((3 * chunk, LANES), BF),
        swap_parts(sent), square, swap,
    )
    mixed, long = call(
        mixing_kernel,
        (shape(field, jnp.float32), like(long)),
        sent, pre_grad, long, bypass, spread,
        far=(0, 1, 2),
        scratch=[pltpu.VMEM(field, BF), pltpu.SemaphoreType.DMA((2,))],
    )
    grad_inputs, grad_bypass = call(
        lambda *refs: columns_back_kernel(*refs, factor=bypass_factor),
        (shape((rows, cols, width), BF), shape((chans, chans), jnp.float32)),
        swap_parts(sent), mixed, square, long,
        keep=False,
    )
    return (grad_inputs, grad_spectral, grad_bypass)


def solution(mesh):
    return jax.shard_map(
        local,
        mesh=mesh,
        in_specs=(
            P("row", "col", None),
            P("row", "col", None),
            P("row", "col", None),
            P(None, "row", "col", None, None),
            P(),
        ),
        out_specs=(P("row", "col", None), P(None, "row", "col", None, None), P()),
        check_vma=False,
    )
```

```python
import math

import jax
import jax.numpy as jnp
import numpy as np
from jax import lax
from jax.experimental import pallas as pl
from jax.experimental.pallas import tpu as pltpu
from jax.sharding import PartitionSpec as P

exact_mode = lax.Precision.HIGHEST


def counting(length):
    return jnp.arange(length, dtype=jnp.int32)


def kept_freq(slot_index, keep_count):
    return jnp.where(slot_index < keep_count // 2, slot_index, slot_index - keep_count)


def phase_table(outer_index, inner_index, length, direction):
    turn_count = jnp.mod(outer_index[:, None] * inner_index[None, :], length)
    angles = turn_count.astype(jnp.float32) * (2.0 * math.pi / length)
    cosine = jnp.cos(angles)
    sine_part = direction * jnp.sin(angles)
    top_rows = jnp.stack([cosine, -sine_part], axis=1)
    low_rows = jnp.stack([sine_part, cosine], axis=1)
    return jnp.stack([top_rows, low_rows], axis=0)


def time_forward(step_count, time_modes):
    turn_count = jnp.mod(counting(step_count)[:, None] * counting(time_modes)[None, :], step_count)
    angles = turn_count.astype(jnp.float32) * (2.0 * math.pi / step_count)
    return jnp.stack([jnp.cos(angles), -jnp.sin(angles)], axis=1)


def time_inverse(step_count, time_modes):
    turn_count = jnp.mod(counting(time_modes)[:, None] * counting(step_count)[None, :], step_count)
    angles = turn_count.astype(jnp.float32) * (2.0 * math.pi / step_count)
    return jnp.stack([jnp.cos(angles), -jnp.sin(angles)], axis=0)


def gelu_slope(values):
    normal_cdf = 0.5 * (1.0 + lax.erf(values * (1.0 / math.sqrt(2.0))))
    density = jnp.exp(-0.5 * values * values) * (1.0 / math.sqrt(2.0 * math.pi))
    return normal_cdf + values * density


def mix_modes(modes_in, modes_grad, weight, factor):
    in_real = modes_in[:, 0]
    in_imag = modes_in[:, 1]
    grad_real = modes_grad[:, 0]
    grad_imag = modes_grad[:, 1]
    real_part = factor * (
        in_real[..., :, None] * grad_real[..., None, :]
        + in_imag[..., :, None] * grad_imag[..., None, :]
    )
    imag_part = factor * (
        in_real[..., :, None] * grad_imag[..., None, :]
        - in_imag[..., :, None] * grad_real[..., None, :]
    )
    weight_grad = jnp.stack([real_part, imag_part], axis=0)
    w_real = weight[0]
    w_imag = weight[1]
    back_real = factor * (
        jnp.einsum("kyscd,kysd->kysc", w_real, grad_real, precision=exact_mode)
        + jnp.einsum("kyscd,kysd->kysc", w_imag, grad_imag, precision=exact_mode)
    )
    back_imag = factor * (
        jnp.einsum("kyscd,kysd->kysc", w_real, grad_imag, precision=exact_mode)
        - jnp.einsum("kyscd,kysd->kysc", w_imag, grad_real, precision=exact_mode)
    )
    return (weight_grad, jnp.stack([back_real, back_imag], axis=1))


def general_local(inputs, preactivation, cotangent, spectral, bypass):
    row_count, col_count, packed = inputs.shape
    chan_count = bypass.shape[0]
    step_count = packed // chan_count
    time_modes = spectral.shape[3]
    owned_row_modes = spectral.shape[1]
    owned_col_modes = spectral.shape[2]
    row_parts = lax.axis_size("row")
    col_parts = lax.axis_size("col")
    row_modes = owned_row_modes * row_parts
    col_modes = owned_col_modes * col_parts
    total_x = row_count * row_parts
    total_y = col_count * col_parts
    factor = 1.0 / math.sqrt(
        float(total_x * total_y * step_count * row_modes * col_modes * time_modes)
    )
    row_start = lax.axis_index("row") * row_count
    col_start = lax.axis_index("col") * col_count
    mode_width = owned_col_modes * time_modes * chan_count
    slopes = gelu_slope(preactivation.astype(jnp.float32))
    pre_grad = (cotangent.astype(jnp.float32) * slopes).astype(jnp.bfloat16)
    flat_inputs = inputs.reshape(-1, chan_count)
    flat_grad = pre_grad.reshape(-1, chan_count)
    local_bypass = jnp.einsum(
        "nc,nd->cd", flat_inputs, flat_grad, preferred_element_type=jnp.float32
    )
    bypass_total = lax.psum(local_bypass, ("row", "col"))
    grad_bypass = bypass_total * (1.0 / math.sqrt(float(total_x * total_y * step_count)))
    forward_t = time_forward(step_count, time_modes)
    col_table = phase_table(counting(col_modes), col_start + counting(col_count), total_y, -1.0)

    def column_terms(field):
        cube_view = field.astype(jnp.float32).reshape(row_count, col_count, step_count, chan_count)
        in_time = jnp.einsum("rytc,tqs->ryqsc", cube_view, forward_t, precision=exact_mode)
        return jnp.einsum("akpy,rypsc->raksc", col_table, in_time, precision=exact_mode)

    col_in, col_grad = (
        lax.psum_scatter(
            column_terms(inputs).astype(jnp.bfloat16), "col", scatter_dimension=2, tiled=True
        ).astype(jnp.float32),
        lax.psum_scatter(
            column_terms(pre_grad).astype(jnp.bfloat16), "col", scatter_dimension=2, tiled=True
        ).astype(jnp.float32),
    )
    flat_in = col_in.reshape(row_count, 2, mode_width)
    flat_cols = col_grad.reshape(row_count, 2, mode_width)
    stacked = jnp.stack([flat_in, flat_cols], axis=2)
    frequencies = kept_freq(counting(owned_row_modes * lax.axis_size("row")), row_modes)
    phases = phase_table(frequencies, row_start + counting(row_count), total_x, -1.0)
    owned_modes = lax.psum_scatter(
        jnp.einsum("akpr,rpbm->kabm", phases, stacked, precision=exact_mode),
        "row",
        scatter_dimension=0,
        tiled=True,
    )
    modes_in = owned_modes[:, :, 0]
    modes_grad = owned_modes[:, :, 1]
    mode_shape = (owned_row_modes, 2, owned_col_modes, time_modes, chan_count)
    weight = spectral.astype(jnp.float32).reshape(
        2, owned_row_modes, owned_col_modes, time_modes, chan_count, chan_count
    )
    weight_grad, back_modes = mix_modes(
        modes_in.reshape(mode_shape), modes_grad.reshape(mode_shape), weight, factor
    )
    grad_spectral = weight_grad.reshape(spectral.shape)
    flat_back = back_modes.reshape(owned_row_modes, 2, mode_width)
    mode_piece = lax.all_gather(flat_back, "row", axis=0, tiled=True)
    span_count = mode_piece.shape[0]
    frequencies = kept_freq(counting(span_count), row_modes)
    phases = phase_table(row_start + counting(row_count), frequencies, total_x, 1.0)
    rows_back = jnp.einsum("axpk,kpm->xam", phases, mode_piece, precision=exact_mode)
    rows_view = rows_back.reshape(row_count, 2, owned_col_modes, time_modes, chan_count)
    col_piece = lax.all_gather(rows_view.astype(jnp.bfloat16), "col", axis=2, tiled=True).astype(
        jnp.float32
    )
    span_count = col_piece.shape[2]
    phases = phase_table(col_start + counting(col_count), counting(span_count), total_y, 1.0)
    cells_y = jnp.zeros(
        (row_count, col_count, 2, time_modes, chan_count), jnp.float32
    ) + jnp.einsum("aypk,rpksc->ryasc", phases, col_piece, precision=exact_mode)
    kernel_grad = jnp.einsum(
        "ryasc,ast->rytc", cells_y, time_inverse(step_count, time_modes), precision=exact_mode
    )
    bypass_grad = jnp.einsum("nd,cd->nc", flat_grad, bypass, preferred_element_type=jnp.float32)
    total_grad = kernel_grad.reshape(-1, chan_count) + bypass_grad
    grad_inputs = total_grad.reshape(inputs.shape).astype(jnp.bfloat16)
    return (grad_inputs, grad_spectral, grad_bypass)


BF = jnp.bfloat16
LANES = 128
SUB = 8


def dot(a, b):
    return jnp.dot(a, b, preferred_element_type=jnp.float32)


def cos_sin(turns, length):
    angles = 2.0 * np.pi * np.mod(turns, length) / length
    return np.cos(angles), np.sin(angles)


def build_tables(parts, rows, cols, steps, chans, row_modes, pair, kept, col_modes, time_modes):
    lead = LANES // chans
    eye = np.eye(chans)
    t_index = np.arange(steps)
    tables = {}
    cos_t, sin_t = cos_sin(np.outer(t_index, np.arange(time_modes)), steps)
    real = [np.kron(cos_t[:, k : k + 1], eye) for k in range(time_modes)]
    imag = [np.kron(-sin_t[:, k : k + 1], eye) for k in range(1, lead)]
    tables["time"] = np.concatenate(real + imag, axis=1)
    ky = np.arange(col_modes)
    y = np.arange(cols)
    cos_y, sin_y = cos_sin(np.outer(ky, y), cols)
    tables["col"] = np.repeat(np.concatenate([cos_y, sin_y], axis=0), rows, axis=0)
    same_row = np.eye(rows)
    col_cos = np.einsum("ky,rs->krsy", cos_y, same_row).reshape(col_modes * rows, rows * cols)
    col_sin = np.einsum("ky,rs->krsy", sin_y, same_row).reshape(col_modes * rows, rows * cols)
    slot = np.arange(row_modes)
    freq = np.where(slot < row_modes // 2, slot, slot - row_modes)
    total_x = parts * rows
    cos_x, sin_x = cos_sin(np.outer(freq, np.arange(total_x)), total_x)
    same_pair = np.eye(pair)

    def spread(matrix):
        blocks = matrix.reshape(parts, kept, parts, rows)
        return np.einsum("ekdr,pq->epkdqr", blocks, same_pair).reshape(
            parts * pair * kept, parts * pair * rows
        )

    tables["row_cos"] = spread(cos_x)
    tables["row_sin"] = spread(sin_x)
    tables["back_cos"] = spread(cos_x).T
    tables["back_sin"] = spread(sin_x).T
    swap = np.kron(np.array([[0.0, -1.0], [1.0, 0.0]]), eye)
    tables["swap"] = np.kron(np.eye(LANES // (2 * chans)), swap)
    order = np.zeros((kept, col_modes, parts, pair, kept))
    for k in range(kept):
        for e in range(parts):
            for p in range(pair):
                order[k, e * pair + p, e, p, k] = 1.0
    tables["order"] = order.reshape(kept * col_modes, parts * pair * kept)
    tables["unorder"] = tables["order"].T
    wide = chans * chans
    repeat = np.kron(eye, np.ones((1, chans)))
    tiled = np.kron(np.ones((1, lead)), eye)
    group = np.zeros((lead + 1, LANES, wide))
    for k in range(lead):
        group[k, k * chans : (k + 1) * chans] = repeat
    extra = np.zeros((LANES, wide))
    extra[chans : 2 * chans] = repeat
    group[lead, :chans] = repeat
    tables["repeat"] = np.concatenate([group, extra[None]], axis=0)
    spots = np.eye(lead)
    tables["tile"] = np.concatenate([np.kron(spots[:, k : k + 1], tiled) for k in range(lead)], axis=1)
    tables["tile_last"] = np.concatenate([np.kron(spots[:, k : k + 1], tiled) for k in (2, 3)], axis=1)
    tables["sums"] = np.tile(repeat.T, (1, lead))
    re_c, re_s = np.kron(cos_t.T, eye), np.kron(sin_t.T, eye)
    cut = lead * chans
    rest = np.zeros((LANES - 2 * chans, steps * chans))
    to_cos = np.concatenate([re_c[:cut], -re_s[:cut], re_c[cut:], -re_s[cut:], rest], axis=0)
    to_sin = np.concatenate([-re_s[:cut], -re_c[:cut], -re_s[cut:], -re_c[cut:], rest], axis=0)
    tables["time_back"] = np.concatenate([to_cos, to_sin], axis=1)
    tables["col_back"] = np.concatenate([col_cos.T, col_sin.T], axis=1)
    place = np.zeros((parts, SUB, chans))
    for c in range(chans):
        place[c, :, c] = 1.0
    tables["place"] = place.reshape(parts * SUB, chans)
    pick = np.zeros((parts, SUB))
    pick[:, 0] = 1.0
    tables["total"] = np.broadcast_to(pick.reshape(1, -1), (parts * SUB, parts * SUB))
    first = np.zeros((chans, parts, SUB))
    for c in range(chans):
        first[c, c, 0] = 1.0
    tables["first"] = first.reshape(chans, parts * SUB)
    tables["spread_chan"] = np.kron(np.ones((steps, 1)), eye)
    return {name: np.asarray(table, np.float32).astype(jnp.bfloat16) for name, table in tables.items()}


def call(kernel, out_shapes, *operands, scratch=(), far=(), limit=12, keep=True):
    near = pl.BlockSpec(memory_space=pltpu.VMEM)
    stay = pl.BlockSpec(memory_space=pltpu.HBM)
    space = lambda i: pltpu.HBM if i in far else pltpu.VMEM
    operands = [pltpu.with_memory_space_constraint(a, space(i)) for i, a in enumerate(operands)]
    hold = lambda a: pltpu.VMEM(a.shape, a.dtype) if keep else a
    return pl.pallas_call(
        kernel,
        out_shape=jax.tree.map(hold, out_shapes),
        in_specs=[stay if i in far else near for i in range(len(operands))],
        out_specs=jax.tree.map(lambda _: near, out_shapes),
        scratch_shapes=list(scratch),
        compiler_params=pltpu.CompilerParams(vmem_limit_bytes=limit * 1024 * 1024),
    )(*operands)


def lane_blocks(values):
    return [values[:, i * LANES : (i + 1) * LANES] for i in range(values.shape[1] // LANES)]


def pack(blocks):
    parts = blocks[0].shape[0] // SUB
    stacked = jnp.concatenate([b.reshape(parts, SUB, LANES) for b in blocks], axis=1)
    return stacked.reshape(-1, LANES).astype(BF)


def unpack(rows, count):
    cube = rows.astype(jnp.float32).reshape(-1, count * SUB, LANES)
    return [cube[:, i * SUB : (i + 1) * SUB].reshape(-1, LANES).astype(BF) for i in range(count)]


def lane_group(shape, chans):
    return lax.broadcasted_iota(jnp.int32, shape, 1) // chans


def halves(values, chans):
    high = values.astype(BF).astype(jnp.float32)
    group = lane_group(values.shape, chans)
    return jnp.where(group == 2, high, jnp.where(group == 3, values - high, 0.0))


def diagonal(values, chans):
    row_step = lax.broadcasted_iota(jnp.int32, values.shape, 0) // chans
    return jnp.where(row_step == lane_group(values.shape, chans), values, 0.0)


def start_copies(sems, *pairs):
    copies = [pltpu.make_async_copy(src, dst, sems.at[i]) for i, (src, dst) in enumerate(pairs)]
    for copy in copies:
        copy.start()
    return copies


def columns_kernel(
    in_hbm, pre_hbm, cot_hbm, time_hbm, col_hbm, square_hbm, swap_hbm, mixing_hbm, sums_hbm, place_hbm,
    out_ref, grad_ref, square_ref, swap_ref, mixing_ref, sums_ref, place_ref,
    in_ref, pre_ref, cot_ref, time_ref, col_ref, sems, *, chans,
):
    copies = start_copies(
        sems,
        (pre_hbm, pre_ref), (cot_hbm, cot_ref), (in_hbm, in_ref), (time_hbm, time_ref), (col_hbm, col_ref),
        (square_hbm, square_ref), (swap_hbm, swap_ref),
        (mixing_hbm, mixing_ref), (sums_hbm, sums_ref), (place_hbm, place_ref),
    )
    rows, cols, width = in_ref.shape
    for copy in copies[:5]:
        copy.wait()
    slopes = gelu_slope(pre_ref[...].reshape(rows * cols, width).astype(jnp.float32))
    grad = (cot_ref[...].reshape(rows * cols, width).astype(jnp.float32) * slopes).astype(BF)
    grad_ref[...] = grad
    field = in_ref[...].reshape(rows * cols, width)
    times = jnp.concatenate([dot(field, time_ref[...]), dot(grad, time_ref[...])], axis=1).astype(BF)
    col = col_ref[...]
    row = lax.broadcasted_iota(jnp.int32, col.shape, 0) % rows
    across = jnp.concatenate([jnp.where(row == r, col, jnp.zeros_like(col)) for r in range(rows)], axis=1)
    waves = dot(across, times)
    half = waves.shape[0] // 2
    in_cos, in_cos2, gr_cos, gr_cos2 = lane_blocks(waves[:half])
    in_sin, in_sin2, gr_sin, gr_sin2 = lane_blocks(waves[half:])
    alone = lane_group(in_cos.shape, chans) == 0
    last = jnp.where(alone, in_cos2, 0.0)
    for place, part in enumerate((-in_sin2, gr_cos2, -gr_sin2)):
        last = last + pltpu.roll(jnp.where(alone, part, 0.0), (place + 1) * chans, 1)
    out_ref[...] = pack(
        [
            in_cos + jnp.where(alone, 0.0, in_sin2),
            jnp.where(alone, 0.0, in_cos2) - in_sin,
            gr_cos + jnp.where(alone, 0.0, gr_sin2),
            jnp.where(alone, 0.0, gr_cos2) - gr_sin,
            last,
        ]
    )
    for copy in copies[5:]:
        copy.wait()


def bypass_terms(field, grad, place, chans):
    products = lax.dot_general(
        field, grad, (((0,), (0,)), ((), ())), preferred_element_type=jnp.float32
    )
    products = diagonal(products, chans)
    partial = products[:chans]
    for step in range(1, field.shape[1] // chans):
        partial = partial + products[step * chans : (step + 1) * chans]
    folded = sum(lane_blocks(partial))
    shift = LANES // 2
    while shift >= chans:
        folded = folded + pltpu.roll(folded, shift, 1)
        shift //= 2
    return dot(place, halves(folded, chans).astype(BF))


def mixing_kernel(
    sent_hbm, grad_hbm, long_hbm, first_hbm, bypass_ref, spread_ref, mixed_ref, long_ref, first_ref, grad_ref, sems
):
    del sent_hbm
    copies = start_copies(sems, (grad_hbm, grad_ref), (long_hbm, long_ref), (first_hbm, first_ref))
    chans = bypass_ref.shape[0]
    spread = spread_ref[...]
    across = lax.dot_general(
        bypass_ref[...], spread, (((0,), (1,)), ((), ())), preferred_element_type=jnp.float32
    ).astype(BF)
    matrix = diagonal(dot(spread, across), chans).astype(BF)
    copies[0].wait()
    mixed_ref[...] = dot(grad_ref[...], matrix)
    for copy in copies[1:]:
        copy.wait()


def rows_kernel(in_ref, square_ref, swap_ref, weight_hbm, out_ref):
    del weight_hbm
    in_re, in_im, gr_re, gr_im, last = unpack(in_ref[...], 5)
    size = square_ref.shape[1]
    turned_last = dot(last, swap_ref[...]).astype(BF)
    direct = jnp.concatenate([in_re, in_im, gr_re, gr_im, last], axis=1)
    turned = jnp.concatenate([in_im, -in_re, gr_im, -gr_re, turned_last], axis=1)
    modes = dot(square_ref[:size], direct) + dot(square_ref[size : 2 * size], turned)
    out_ref[...] = pack(lane_blocks(modes))


def mixing_tables(table_ref):
    size = table_ref.shape[1]
    tiles = [table_ref[2 * size + i * LANES : 2 * size + (i + 1) * LANES] for i in range(3)]
    return table_ref[:size], table_ref[size : 2 * size], *tiles


def back_kernel(
    in_ref, grad_ref, weight_ref, field_ref, table_ref, sums_ref, place_ref, repeat_hbm, rows_hbm,
    out_ref, modes_ref, repeat_ref, rows_ref, sems, *, factor,
):
    chans = place_ref.shape[1]
    copies = start_copies(sems, (rows_hbm, rows_ref), (repeat_hbm, repeat_ref))
    size = table_ref.shape[1]
    order, unorder, tile_a, tile_b, tile_last = mixing_tables(table_ref)
    lanes = jnp.concatenate(unpack(in_ref[...], 5), axis=1)
    modes = dot(order, lanes).astype(BF)
    modes_ref[...] = modes
    steps = weight_ref.shape[2]
    wide = weight_ref.shape[4]
    lead = LANES // chans
    gr_re, gr_im, last = lane_blocks(modes)[2:]
    first = jnp.concatenate([gr_re, gr_im], axis=1)
    blank = jnp.zeros((LANES, LANES), BF)
    tiles = [
        jnp.concatenate([jnp.concatenate([t, blank], axis=1), jnp.concatenate([blank, t], axis=1)], axis=0)
        for t in lane_blocks(tile_a) + lane_blocks(tile_b)
    ]
    group = lane_group((size, LANES), chans)
    re_sum = im_sum = jnp.zeros((size, LANES), jnp.float32)
    for k in range(steps):
        g_re, g_im = lane_blocks((dot(first, tiles[k]) if k < lead else dot(last, tile_last)).astype(BF))
        p_re, p_im = [], []
        for j in range(wide // LANES):
            w_re = weight_ref[0, :, k, :, j * LANES : (j + 1) * LANES].reshape(size, LANES)
            w_im = weight_ref[1, :, k, :, j * LANES : (j + 1) * LANES].reshape(size, LANES)
            p_re.append(w_re * g_re + w_im * g_im)
            p_im.append(w_re * g_im - w_im * g_re)
        both = jnp.concatenate([jnp.concatenate(p_re, axis=1), jnp.concatenate(p_im, axis=1)], axis=0)
        summed = dot(both, sums_ref[...])
        if k < lead:
            re_sum = jnp.where(group == k, summed[:size], re_sum)
            im_sum = jnp.where(group == k, summed[size:], im_sum)
        else:
            last_sum = jnp.where(group == 0, summed[:size], jnp.where(group == 1, summed[size:], 0.0))
    rows, cols, width = field_ref.shape
    terms = bypass_terms(field_ref[...].reshape(rows * cols, width), grad_ref[...], place_ref[...], chans)
    back = (jnp.concatenate([re_sum, im_sum, last_sum], axis=1) * factor).astype(BF)
    re, im, last = lane_blocks(dot(unorder, back))
    out_ref[...] = pack([re, im, last + terms])
    for copy in copies:
        copy.wait()


def weight_kernel(modes_ref, repeat_ref, table_ref, out_hbm, out_ref, sems, *, factor):
    slots, _, kept, count, wide = out_ref.shape
    steps = out_hbm.shape[2]
    lead = repeat_ref.shape[0] - 2
    in_re, in_im, gr_re, gr_im, last = lane_blocks(modes_ref[...])
    _, _, tile_a, tile_b, tile_last = mixing_tables(table_ref)
    tiled = [lane_blocks(dot(g, tile_a) * factor) + lane_blocks(dot(g, tile_b) * factor) for g in (gr_re, gr_im)]
    tiled = list(zip(*tiled)) + [lane_blocks(dot(last, tile_last) * factor)]
    copies = []
    for k in range(steps):
        if k < lead:
            a_re, a_im = dot(in_re, repeat_ref[k]), dot(in_im, repeat_ref[k])
        else:
            a_re, a_im = dot(last, repeat_ref[lead]), dot(last, repeat_ref[lead + 1])
        b_re, b_im = tiled[k]
        slot = k % slots
        if k >= slots:
            copies[k - slots].wait()
        for j in range(wide // LANES):
            part = slice(j * LANES, (j + 1) * LANES)
            out_ref[slot, 0, :, :, part] = (a_re[:, part] * b_re + a_im[:, part] * b_im).reshape(kept, count, LANES)
            out_ref[slot, 1, :, :, part] = (a_re[:, part] * b_im - a_im[:, part] * b_re).reshape(kept, count, LANES)
        copies.append(pltpu.make_async_copy(out_ref.at[slot], out_hbm.at[:, :, k], sems.at[slot]))
        copies[k].start()
    for copy in copies[max(0, steps - slots) :]:
        copy.wait()


def rows_back_kernel(in_ref, table_ref, swap_ref, out_ref, *, chans):
    re, im, tail = unpack(in_ref[...], 3)
    size = table_ref.shape[1]
    back_cos, back_sin, total = [table_ref[i * size : (i + 1) * size] for i in range(3)]
    group = lane_group(tail.shape, chans)
    last = jnp.where(group < 2, tail.astype(jnp.float32), 0.0).astype(BF)
    turned_last = dot(-last, swap_ref[...]).astype(BF)
    direct = jnp.concatenate([re, im, last], axis=1)
    turned = jnp.concatenate([-im, re, turned_last], axis=1)
    rows = dot(back_cos, direct) + dot(back_sin, turned)
    summed = dot(total, tail)
    summed = summed + pltpu.roll(summed, LANES - chans, 1)
    summed = jnp.where(group == 2, summed, 0.0)
    summed = summed + pltpu.roll(summed, chans, 1)
    re, im, last = lane_blocks(rows)
    out_ref[...] = pack([re, im, last + halves(summed, chans)])


def columns_back_kernel(in_ref, mixed_ref, first_ref, long_ref, out_ref, bypass_ref, *, factor):
    rows, cols, width = out_ref.shape
    chans = bypass_ref.shape[0]
    blocks = unpack(in_ref[...], 3)
    lanes = jnp.concatenate(blocks, axis=1)
    height = lanes.shape[1]
    steps = dot(lanes, long_ref[:height]).astype(BF)
    stacked = jnp.concatenate([steps[:, :width], steps[:, width:]], axis=0)
    total = dot(long_ref[height:], stacked) + mixed_ref[...]
    out_ref[...] = total.reshape(rows, cols, width).astype(BF)
    sums = dot(first_ref[...], blocks[2])
    sums = pltpu.roll(sums + pltpu.roll(sums, LANES - chans, 1), LANES // 2, 1)
    bypass_ref[...] = sums[:, :chans] * factor


def local(inputs, preactivation, cotangent, spectral, bypass):
    rows, cols, width = inputs.shape
    chans = bypass.shape[0]
    steps = width // chans
    kept, col_modes, time_modes, wide = spectral.shape[1:]
    parts = lax.axis_size("row")
    pair = col_modes // parts
    fits = (
        lax.axis_size("col") == 1
        and col_modes % parts == 0
        and pair * rows == SUB
        and pair * kept == SUB
        and parts == chans
        and 4 * chans == LANES
        and time_modes == 5
        and steps == 8
        and cols % LANES == 0
    )
    if not fits:
        return general_local(inputs, preactivation, cotangent, spectral, bypass)
    row_modes = kept * parts
    total_x = rows * parts
    factor = 1.0 / math.sqrt(float(total_x * cols * steps * row_modes * col_modes * time_modes))
    bypass_factor = 1.0 / math.sqrt(float(total_x * cols * steps))
    tables = build_tables(parts, rows, cols, steps, chans, row_modes, pair, kept, col_modes, time_modes)
    stack_all = lambda arrays: jnp.asarray(np.concatenate(arrays, axis=0))
    stack = lambda *names: stack_all([tables[name] for name in names])
    square = stack("row_cos", "row_sin")
    mixing = stack_all(
        [tables["order"], tables["unorder"]] + np.split(tables["tile"], 2, axis=1) + [tables["tile_last"]]
    )
    back_table = stack("back_cos", "back_sin", "total")
    long = stack("time_back", "col_back")
    time_table, col_table, swap, repeat, sums, spread, place, first = [
        jnp.asarray(tables[name])
        for name in ("time", "col", "swap", "repeat", "sums", "spread_chan", "place", "first")
    ]

    def swap_parts(array):
        return lax.all_to_all(array, "row", 0, 0, tiled=True)

    like = lambda array: jax.ShapeDtypeStruct(array.shape, array.dtype)
    shape = jax.ShapeDtypeStruct
    chunk = parts * SUB
    field = (rows * cols, width)
    sent, pre_grad, square, swap, mixing, sums, place = call(
        lambda *refs: columns_kernel(*refs, chans=chans),
        (shape((5 * chunk, LANES), BF), shape(field, BF))
        + tuple(like(a) for a in (square, swap, mixing, sums, place)),
        inputs, preactivation, cotangent, time_table, col_table, square, swap, mixing, sums, place,
        far=range(10),
        scratch=[pltpu.VMEM(a.shape, a.dtype) for a in (inputs, inputs, inputs, time_table, col_table)]
        + [pltpu.SemaphoreType.DMA((10,))],
    )
    weight = spectral.transpose(0, 1, 3, 2, 4)
    sent = call(rows_kernel, shape((5 * chunk, LANES), BF), swap_parts(sent), square, swap, weight, far=(3,))
    sent, modes, repeat, back_table = call(
        lambda *refs: back_kernel(*refs, factor=factor),
        (shape((3 * chunk, LANES), BF), shape((kept * col_modes, 5 * LANES), BF), like(repeat), like(back_table)),
        swap_parts(sent), pre_grad, weight, inputs, mixing, sums, place, repeat, back_table,
        far=(7, 8),
        scratch=[pltpu.SemaphoreType.DMA((2,))],
    )
    near = pl.BlockSpec(memory_space=pltpu.VMEM)
    slots = 3
    grad_spectral = pl.pallas_call(
        lambda *refs: weight_kernel(*refs, factor=factor),
        out_shape=shape((2, kept, time_modes, col_modes, wide), jnp.float32),
        in_specs=[near, near, near],
        out_specs=pl.BlockSpec(memory_space=pltpu.HBM),
        scratch_shapes=[
            pltpu.VMEM((slots, 2, kept, col_modes, wide), jnp.float32), pltpu.SemaphoreType.DMA((slots,)),
        ],
        compiler_params=pltpu.CompilerParams(vmem_limit_bytes=16 * 1024 * 1024),
    )(*[pltpu.with_memory_space_constraint(a, pltpu.VMEM) for a in (modes, repeat, mixing)]).transpose(0, 1, 3, 2, 4)
    sent = call(
        lambda *refs: rows_back_kernel(*refs, chans=chans),
        shape((3 * chunk, LANES), BF),
        swap_parts(sent), back_table, swap,
    )
    mixed, long, first = call(
        mixing_kernel,
        (shape(field, jnp.float32), like(long), like(first)),
        sent, pre_grad, long, first, bypass, spread,
        far=(0, 1, 2, 3),
        scratch=[pltpu.VMEM(field, BF), pltpu.SemaphoreType.DMA((3,))],
    )
    grad_inputs, grad_bypass = call(
        lambda *refs: columns_back_kernel(*refs, factor=bypass_factor),
        (shape((rows, cols, width), BF), shape((chans, chans), jnp.float32)),
        swap_parts(sent), mixed, first, long,
        keep=False,
    )
    return (grad_inputs, grad_spectral, grad_bypass)


def solution(mesh):
    return jax.shard_map(
        local,
        mesh=mesh,
        in_specs=(
            P("row", "col", None),
            P("row", "col", None),
            P("row", "col", None),
            P(None, "row", "col", None, None),
            P(),
        ),
        out_specs=(P("row", "col", None), P(None, "row", "col", None, None), P()),
        check_vma=False,
    )
```

```python
import math

import jax
import jax.numpy as jnp
import numpy as np
from jax import lax
from jax.experimental import pallas as pl
from jax.experimental.pallas import tpu as pltpu
from jax.sharding import PartitionSpec as P

exact_mode = lax.Precision.HIGHEST


def counting(length):
    return jnp.arange(length, dtype=jnp.int32)


def kept_freq(slot_index, keep_count):
    return jnp.where(slot_index < keep_count // 2, slot_index, slot_index - keep_count)


def phase_table(outer_index, inner_index, length, direction):
    turn_count = jnp.mod(outer_index[:, None] * inner_index[None, :], length)
    angles = turn_count.astype(jnp.float32) * (2.0 * math.pi / length)
    cosine = jnp.cos(angles)
    sine_part = direction * jnp.sin(angles)
    top_rows = jnp.stack([cosine, -sine_part], axis=1)
    low_rows = jnp.stack([sine_part, cosine], axis=1)
    return jnp.stack([top_rows, low_rows], axis=0)


def time_forward(step_count, time_modes):
    turn_count = jnp.mod(counting(step_count)[:, None] * counting(time_modes)[None, :], step_count)
    angles = turn_count.astype(jnp.float32) * (2.0 * math.pi / step_count)
    return jnp.stack([jnp.cos(angles), -jnp.sin(angles)], axis=1)


def time_inverse(step_count, time_modes):
    turn_count = jnp.mod(counting(time_modes)[:, None] * counting(step_count)[None, :], step_count)
    angles = turn_count.astype(jnp.float32) * (2.0 * math.pi / step_count)
    return jnp.stack([jnp.cos(angles), -jnp.sin(angles)], axis=0)


def gelu_slope(values):
    normal_cdf = 0.5 * (1.0 + lax.erf(values * (1.0 / math.sqrt(2.0))))
    density = jnp.exp(-0.5 * values * values) * (1.0 / math.sqrt(2.0 * math.pi))
    return normal_cdf + values * density


def mix_modes(modes_in, modes_grad, weight, factor):
    in_real = modes_in[:, 0]
    in_imag = modes_in[:, 1]
    grad_real = modes_grad[:, 0]
    grad_imag = modes_grad[:, 1]
    real_part = factor * (
        in_real[..., :, None] * grad_real[..., None, :]
        + in_imag[..., :, None] * grad_imag[..., None, :]
    )
    imag_part = factor * (
        in_real[..., :, None] * grad_imag[..., None, :]
        - in_imag[..., :, None] * grad_real[..., None, :]
    )
    weight_grad = jnp.stack([real_part, imag_part], axis=0)
    w_real = weight[0]
    w_imag = weight[1]
    back_real = factor * (
        jnp.einsum("kyscd,kysd->kysc", w_real, grad_real, precision=exact_mode)
        + jnp.einsum("kyscd,kysd->kysc", w_imag, grad_imag, precision=exact_mode)
    )
    back_imag = factor * (
        jnp.einsum("kyscd,kysd->kysc", w_real, grad_imag, precision=exact_mode)
        - jnp.einsum("kyscd,kysd->kysc", w_imag, grad_real, precision=exact_mode)
    )
    return (weight_grad, jnp.stack([back_real, back_imag], axis=1))


def general_local(inputs, preactivation, cotangent, spectral, bypass):
    row_count, col_count, packed = inputs.shape
    chan_count = bypass.shape[0]
    step_count = packed // chan_count
    time_modes = spectral.shape[3]
    owned_row_modes = spectral.shape[1]
    owned_col_modes = spectral.shape[2]
    row_parts = lax.axis_size("row")
    col_parts = lax.axis_size("col")
    row_modes = owned_row_modes * row_parts
    col_modes = owned_col_modes * col_parts
    total_x = row_count * row_parts
    total_y = col_count * col_parts
    factor = 1.0 / math.sqrt(
        float(total_x * total_y * step_count * row_modes * col_modes * time_modes)
    )
    row_start = lax.axis_index("row") * row_count
    col_start = lax.axis_index("col") * col_count
    mode_width = owned_col_modes * time_modes * chan_count
    slopes = gelu_slope(preactivation.astype(jnp.float32))
    pre_grad = (cotangent.astype(jnp.float32) * slopes).astype(jnp.bfloat16)
    flat_inputs = inputs.reshape(-1, chan_count)
    flat_grad = pre_grad.reshape(-1, chan_count)
    local_bypass = jnp.einsum(
        "nc,nd->cd", flat_inputs, flat_grad, preferred_element_type=jnp.float32
    )
    bypass_total = lax.psum(local_bypass, ("row", "col"))
    grad_bypass = bypass_total * (1.0 / math.sqrt(float(total_x * total_y * step_count)))
    forward_t = time_forward(step_count, time_modes)
    col_table = phase_table(counting(col_modes), col_start + counting(col_count), total_y, -1.0)

    def column_terms(field):
        cube_view = field.astype(jnp.float32).reshape(row_count, col_count, step_count, chan_count)
        in_time = jnp.einsum("rytc,tqs->ryqsc", cube_view, forward_t, precision=exact_mode)
        return jnp.einsum("akpy,rypsc->raksc", col_table, in_time, precision=exact_mode)

    col_in, col_grad = (
        lax.psum_scatter(
            column_terms(inputs).astype(jnp.bfloat16), "col", scatter_dimension=2, tiled=True
        ).astype(jnp.float32),
        lax.psum_scatter(
            column_terms(pre_grad).astype(jnp.bfloat16), "col", scatter_dimension=2, tiled=True
        ).astype(jnp.float32),
    )
    flat_in = col_in.reshape(row_count, 2, mode_width)
    flat_cols = col_grad.reshape(row_count, 2, mode_width)
    stacked = jnp.stack([flat_in, flat_cols], axis=2)
    frequencies = kept_freq(counting(owned_row_modes * lax.axis_size("row")), row_modes)
    phases = phase_table(frequencies, row_start + counting(row_count), total_x, -1.0)
    owned_modes = lax.psum_scatter(
        jnp.einsum("akpr,rpbm->kabm", phases, stacked, precision=exact_mode),
        "row",
        scatter_dimension=0,
        tiled=True,
    )
    modes_in = owned_modes[:, :, 0]
    modes_grad = owned_modes[:, :, 1]
    mode_shape = (owned_row_modes, 2, owned_col_modes, time_modes, chan_count)
    weight = spectral.astype(jnp.float32).reshape(
        2, owned_row_modes, owned_col_modes, time_modes, chan_count, chan_count
    )
    weight_grad, back_modes = mix_modes(
        modes_in.reshape(mode_shape), modes_grad.reshape(mode_shape), weight, factor
    )
    grad_spectral = weight_grad.reshape(spectral.shape)
    flat_back = back_modes.reshape(owned_row_modes, 2, mode_width)
    mode_piece = lax.all_gather(flat_back, "row", axis=0, tiled=True)
    span_count = mode_piece.shape[0]
    frequencies = kept_freq(counting(span_count), row_modes)
    phases = phase_table(row_start + counting(row_count), frequencies, total_x, 1.0)
    rows_back = jnp.einsum("axpk,kpm->xam", phases, mode_piece, precision=exact_mode)
    rows_view = rows_back.reshape(row_count, 2, owned_col_modes, time_modes, chan_count)
    col_piece = lax.all_gather(rows_view.astype(jnp.bfloat16), "col", axis=2, tiled=True).astype(
        jnp.float32
    )
    span_count = col_piece.shape[2]
    phases = phase_table(col_start + counting(col_count), counting(span_count), total_y, 1.0)
    cells_y = jnp.zeros(
        (row_count, col_count, 2, time_modes, chan_count), jnp.float32
    ) + jnp.einsum("aypk,rpksc->ryasc", phases, col_piece, precision=exact_mode)
    kernel_grad = jnp.einsum(
        "ryasc,ast->rytc", cells_y, time_inverse(step_count, time_modes), precision=exact_mode
    )
    bypass_grad = jnp.einsum("nd,cd->nc", flat_grad, bypass, preferred_element_type=jnp.float32)
    total_grad = kernel_grad.reshape(-1, chan_count) + bypass_grad
    grad_inputs = total_grad.reshape(inputs.shape).astype(jnp.bfloat16)
    return (grad_inputs, grad_spectral, grad_bypass)


BF = jnp.bfloat16
LANES = 128
SUB = 8


def dot(a, b):
    return jnp.dot(a, b, preferred_element_type=jnp.float32)


def cos_sin(turns, length):
    angles = 2.0 * np.pi * np.mod(turns, length) / length
    return np.cos(angles), np.sin(angles)


def build_tables(parts, rows, cols, steps, chans, row_modes, pair, kept, col_modes, time_modes):
    lead = LANES // chans
    eye = np.eye(chans)
    t_index = np.arange(steps)
    tables = {}
    cos_t, sin_t = cos_sin(np.outer(t_index, np.arange(time_modes)), steps)
    real = [np.kron(cos_t[:, k : k + 1], eye) for k in range(time_modes)]
    imag = [np.kron(-sin_t[:, k : k + 1], eye) for k in range(1, lead)]
    tables["time"] = np.concatenate(real + imag, axis=1)
    ky = np.arange(col_modes)
    y = np.arange(cols)
    cos_y, sin_y = cos_sin(np.outer(ky, y), cols)
    tables["col"] = np.repeat(np.concatenate([cos_y, sin_y], axis=0), rows, axis=0)
    same_row = np.eye(rows)
    col_cos = np.einsum("ky,rs->krsy", cos_y, same_row).reshape(col_modes * rows, rows * cols)
    col_sin = np.einsum("ky,rs->krsy", sin_y, same_row).reshape(col_modes * rows, rows * cols)
    slot = np.arange(row_modes)
    freq = np.where(slot < row_modes // 2, slot, slot - row_modes)
    total_x = parts * rows
    cos_x, sin_x = cos_sin(np.outer(freq, np.arange(total_x)), total_x)
    same_pair = np.eye(pair)

    def spread(matrix):
        blocks = matrix.reshape(parts, kept, parts, rows)
        return np.einsum("ekdr,pq->epkdqr", blocks, same_pair).reshape(
            parts * pair * kept, parts * pair * rows
        )

    tables["row_cos"] = spread(cos_x)
    tables["row_sin"] = spread(sin_x)
    tables["back_cos"] = spread(cos_x).T
    tables["back_sin"] = spread(sin_x).T
    order = np.zeros((kept, col_modes, parts, pair, kept))
    for k in range(kept):
        for e in range(parts):
            for p in range(pair):
                order[k, e * pair + p, e, p, k] = 1.0
    tables["order"] = order.reshape(kept * col_modes, parts * pair * kept)
    tables["unorder"] = tables["order"].T
    wide = chans * chans
    repeat = np.kron(eye, np.ones((1, chans)))
    tiled = np.kron(np.ones((1, lead)), eye)
    group = np.zeros((lead + 1, LANES, wide))
    for k in range(lead):
        group[k, k * chans : (k + 1) * chans] = repeat
    extra = np.zeros((LANES, wide))
    extra[chans : 2 * chans] = repeat
    group[lead, :chans] = repeat
    tables["repeat"] = np.concatenate([group, extra[None]], axis=0)
    spots = np.eye(lead)
    tables["tile"] = np.concatenate([np.kron(spots[:, k : k + 1], tiled) for k in range(lead)], axis=1)
    tables["tile_last"] = np.concatenate([np.kron(spots[:, k : k + 1], tiled) for k in (2, 3)], axis=1)
    tables["sums"] = np.tile(repeat.T, (1, lead))
    re_c, re_s = np.kron(cos_t.T, eye), np.kron(sin_t.T, eye)
    cut = lead * chans
    rest = np.zeros((LANES - 2 * chans, steps * chans))
    to_cos = np.concatenate([re_c[:cut], -re_s[:cut], re_c[cut:], -re_s[cut:], rest], axis=0)
    to_sin = np.concatenate([-re_s[:cut], -re_c[:cut], -re_s[cut:], -re_c[cut:], rest], axis=0)
    tables["time_back"] = np.concatenate([to_cos, to_sin], axis=1)
    tables["col_back"] = np.concatenate([col_cos.T, col_sin.T], axis=1)
    place = np.zeros((parts, SUB, chans))
    for c in range(chans):
        place[c, :, c] = 1.0
    tables["place"] = place.reshape(parts * SUB, chans)
    pick = np.zeros((parts, SUB))
    pick[:, 0] = 1.0
    tables["total"] = np.broadcast_to(pick.reshape(1, -1), (parts * SUB, parts * SUB))
    first = np.zeros((chans, parts, SUB))
    for c in range(chans):
        first[c, c, 0] = 1.0
    tables["first"] = first.reshape(chans, parts * SUB)
    tables["spread_chan"] = np.kron(np.ones((steps, 1)), eye)
    return {name: np.asarray(table, np.float32).astype(jnp.bfloat16) for name, table in tables.items()}


def call(kernel, out_shapes, *operands, scratch=(), far=(), limit=12, keep=True):
    near = pl.BlockSpec(memory_space=pltpu.VMEM)
    stay = pl.BlockSpec(memory_space=pltpu.HBM)
    space = lambda i: pltpu.HBM if i in far else pltpu.VMEM
    operands = [pltpu.with_memory_space_constraint(a, space(i)) for i, a in enumerate(operands)]
    hold = lambda a: pltpu.VMEM(a.shape, a.dtype) if keep else a
    return pl.pallas_call(
        kernel,
        out_shape=jax.tree.map(hold, out_shapes),
        in_specs=[stay if i in far else near for i in range(len(operands))],
        out_specs=jax.tree.map(lambda _: near, out_shapes),
        scratch_shapes=list(scratch),
        compiler_params=pltpu.CompilerParams(vmem_limit_bytes=limit * 1024 * 1024),
    )(*operands)


def lane_blocks(values):
    return [values[:, i * LANES : (i + 1) * LANES] for i in range(values.shape[1] // LANES)]


def pack(blocks):
    parts = blocks[0].shape[0] // SUB
    stacked = jnp.concatenate([b.reshape(parts, SUB, LANES) for b in blocks], axis=1)
    return stacked.reshape(-1, LANES).astype(BF)


def unpack(rows, count):
    cube = rows.astype(jnp.float32).reshape(-1, count * SUB, LANES)
    return [cube[:, i * SUB : (i + 1) * SUB].reshape(-1, LANES).astype(BF) for i in range(count)]


def lane_group(shape, chans):
    return lax.broadcasted_iota(jnp.int32, shape, 1) // chans


def halves(values, chans):
    high = values.astype(BF).astype(jnp.float32)
    group = lane_group(values.shape, chans)
    return jnp.where(group == 2, high, jnp.where(group == 3, values - high, 0.0))


def diagonal(values, chans):
    row_step = lax.broadcasted_iota(jnp.int32, values.shape, 0) // chans
    return jnp.where(row_step == lane_group(values.shape, chans), values, 0.0)


def start_copies(sems, *pairs):
    copies = [pltpu.make_async_copy(src, dst, sems.at[i]) for i, (src, dst) in enumerate(pairs)]
    for copy in copies:
        copy.start()
    return copies


def columns_kernel(
    in_hbm, pre_hbm, cot_hbm, time_hbm, col_hbm, square_hbm,
    out_ref, grad_ref, square_ref,
    in_ref, pre_ref, cot_ref, time_ref, col_ref, sems, *, chans,
):
    copies = start_copies(
        sems,
        (pre_hbm, pre_ref), (cot_hbm, cot_ref), (in_hbm, in_ref), (time_hbm, time_ref), (col_hbm, col_ref),
        (square_hbm, square_ref),
    )
    rows, cols, width = in_ref.shape
    for copy in copies[:5]:
        copy.wait()
    slopes = gelu_slope(pre_ref[...].reshape(rows * cols, width).astype(jnp.float32))
    grad = (cot_ref[...].reshape(rows * cols, width).astype(jnp.float32) * slopes).astype(BF)
    grad_ref[...] = grad
    field = in_ref[...].reshape(rows * cols, width)
    times = jnp.concatenate([dot(field, time_ref[...]), dot(grad, time_ref[...])], axis=1).astype(BF)
    col = col_ref[...]
    row = lax.broadcasted_iota(jnp.int32, col.shape, 0) % rows
    across = jnp.concatenate([jnp.where(row == r, col, jnp.zeros_like(col)) for r in range(rows)], axis=1)
    waves = dot(across, times)
    half = waves.shape[0] // 2
    in_cos, in_cos2, gr_cos, gr_cos2 = lane_blocks(waves[:half])
    in_sin, in_sin2, gr_sin, gr_sin2 = lane_blocks(waves[half:])
    alone = lane_group(in_cos.shape, chans) == 0
    last = jnp.where(alone, in_cos2, 0.0)
    for place, part in enumerate((-in_sin2, gr_cos2, -gr_sin2)):
        last = last + pltpu.roll(jnp.where(alone, part, 0.0), (place + 1) * chans, 1)
    out_ref[...] = pack(
        [
            in_cos + jnp.where(alone, 0.0, in_sin2),
            jnp.where(alone, 0.0, in_cos2) - in_sin,
            gr_cos + jnp.where(alone, 0.0, gr_sin2),
            jnp.where(alone, 0.0, gr_cos2) - gr_sin,
            last,
        ]
    )
    for copy in copies[5:]:
        copy.wait()


def bypass_terms(field, grad, place, chans):
    products = lax.dot_general(
        field, grad, (((0,), (0,)), ((), ())), preferred_element_type=jnp.float32
    )
    products = diagonal(products, chans)
    partial = products[:chans]
    for step in range(1, field.shape[1] // chans):
        partial = partial + products[step * chans : (step + 1) * chans]
    folded = sum(lane_blocks(partial))
    shift = LANES // 2
    while shift >= chans:
        folded = folded + pltpu.roll(folded, shift, 1)
        shift //= 2
    return dot(place, halves(folded, chans).astype(BF))


def mixing_kernel(
    sent_hbm, grad_hbm, long_hbm, first_hbm, bypass_ref, spread_ref, mixed_ref, long_ref, first_ref, grad_ref, sems
):
    del sent_hbm
    copies = start_copies(sems, (grad_hbm, grad_ref), (long_hbm, long_ref), (first_hbm, first_ref))
    chans = bypass_ref.shape[0]
    spread = spread_ref[...]
    across = lax.dot_general(
        bypass_ref[...], spread, (((0,), (1,)), ((), ())), preferred_element_type=jnp.float32
    ).astype(BF)
    matrix = diagonal(dot(spread, across), chans).astype(BF)
    copies[0].wait()
    mixed_ref[...] = dot(grad_ref[...], matrix)
    for copy in copies[1:]:
        copy.wait()


def quarter_turn(values, chans):
    ahead, behind = pltpu.roll(values, LANES - chans, 1), pltpu.roll(values, chans, 1)
    return jnp.where(lane_group(values.shape, chans) % 2 == 0, ahead, -behind)


def rows_kernel(in_ref, square_ref, weight_hbm, out_ref, *, chans):
    del weight_hbm
    in_re, in_im, gr_re, gr_im, last = unpack(in_ref[...], 5)
    size = square_ref.shape[1]
    turned_last = quarter_turn(last.astype(jnp.float32), chans).astype(BF)
    direct = jnp.concatenate([in_re, in_im, gr_re, gr_im, last], axis=1)
    turned = jnp.concatenate([in_im, -in_re, gr_im, -gr_re, turned_last], axis=1)
    modes = dot(square_ref[:size], direct) + dot(square_ref[size : 2 * size], turned)
    out_ref[...] = pack(lane_blocks(modes))


def mixing_tables(table_ref):
    size = table_ref.shape[1]
    tiles = [table_ref[2 * size + i * LANES : 2 * size + (i + 1) * LANES] for i in range(3)]
    return table_ref[:size], table_ref[size : 2 * size], *tiles


def back_kernel(
    in_ref, grad_ref, weight_ref, field_ref, table_ref, sums_ref, place_ref, repeat_hbm, rows_hbm,
    out_ref, modes_ref, repeat_ref, rows_ref, sems, *, factor,
):
    chans = place_ref.shape[1]
    copies = start_copies(sems, (rows_hbm, rows_ref), (repeat_hbm, repeat_ref))
    size = table_ref.shape[1]
    order, unorder, tile_a, tile_b, tile_last = mixing_tables(table_ref)
    lanes = jnp.concatenate(unpack(in_ref[...], 5), axis=1)
    modes = dot(order, lanes).astype(BF)
    modes_ref[...] = modes
    steps = weight_ref.shape[2]
    wide = weight_ref.shape[4]
    lead = LANES // chans
    gr_re, gr_im, last = lane_blocks(modes)[2:]
    first = jnp.concatenate([gr_re, gr_im], axis=1)
    blank = jnp.zeros((LANES, LANES), BF)
    tiles = [
        jnp.concatenate([jnp.concatenate([t, blank], axis=1), jnp.concatenate([blank, t], axis=1)], axis=0)
        for t in lane_blocks(tile_a) + lane_blocks(tile_b)
    ]
    group = lane_group((size, LANES), chans)
    re_sum = im_sum = jnp.zeros((size, LANES), jnp.float32)
    for k in range(steps):
        g_re, g_im = lane_blocks((dot(first, tiles[k]) if k < lead else dot(last, tile_last)).astype(BF))
        p_re, p_im = [], []
        for j in range(wide // LANES):
            w_re = weight_ref[0, :, k, :, j * LANES : (j + 1) * LANES].reshape(size, LANES)
            w_im = weight_ref[1, :, k, :, j * LANES : (j + 1) * LANES].reshape(size, LANES)
            p_re.append(w_re * g_re + w_im * g_im)
            p_im.append(w_re * g_im - w_im * g_re)
        both = jnp.concatenate([jnp.concatenate(p_re, axis=1), jnp.concatenate(p_im, axis=1)], axis=0)
        summed = dot(both, sums_ref[...])
        if k < lead:
            re_sum = jnp.where(group == k, summed[:size], re_sum)
            im_sum = jnp.where(group == k, summed[size:], im_sum)
        else:
            last_sum = jnp.where(group == 0, summed[:size], jnp.where(group == 1, summed[size:], 0.0))
    rows, cols, width = field_ref.shape
    terms = bypass_terms(field_ref[...].reshape(rows * cols, width), grad_ref[...], place_ref[...], chans)
    back = (jnp.concatenate([re_sum, im_sum, last_sum], axis=1) * factor).astype(BF)
    re, im, last = lane_blocks(dot(unorder, back))
    out_ref[...] = pack([re, im, last + terms])
    for copy in copies:
        copy.wait()


def weight_kernel(modes_ref, repeat_ref, table_ref, out_hbm, out_ref, sems, *, factor):
    slots, _, kept, count, wide = out_ref.shape
    steps = out_hbm.shape[2]
    lead = repeat_ref.shape[0] - 2
    in_re, in_im, gr_re, gr_im, last = lane_blocks(modes_ref[...])
    _, _, tile_a, tile_b, tile_last = mixing_tables(table_ref)
    tiled = [lane_blocks(dot(g, tile_a) * factor) + lane_blocks(dot(g, tile_b) * factor) for g in (gr_re, gr_im)]
    tiled = list(zip(*tiled)) + [lane_blocks(dot(last, tile_last) * factor)]
    copies = []
    for k in range(steps):
        if k < lead:
            a_re, a_im = dot(in_re, repeat_ref[k]), dot(in_im, repeat_ref[k])
        else:
            a_re, a_im = dot(last, repeat_ref[lead]), dot(last, repeat_ref[lead + 1])
        b_re, b_im = tiled[k]
        slot = k % slots
        if k >= slots:
            copies[k - slots].wait()
        for j in range(wide // LANES):
            part = slice(j * LANES, (j + 1) * LANES)
            out_ref[slot, 0, :, :, part] = (a_re[:, part] * b_re + a_im[:, part] * b_im).reshape(kept, count, LANES)
            out_ref[slot, 1, :, :, part] = (a_re[:, part] * b_im - a_im[:, part] * b_re).reshape(kept, count, LANES)
        copies.append(pltpu.make_async_copy(out_ref.at[slot], out_hbm.at[:, :, k], sems.at[slot]))
        copies[k].start()
    for copy in copies[max(0, steps - slots) :]:
        copy.wait()


def rows_back_kernel(in_ref, table_ref, out_ref, *, chans):
    re, im, tail = unpack(in_ref[...], 3)
    size = table_ref.shape[1]
    back_cos, back_sin, total = [table_ref[i * size : (i + 1) * size] for i in range(3)]
    group = lane_group(tail.shape, chans)
    last = jnp.where(group < 2, tail.astype(jnp.float32), 0.0)
    turned_last = -quarter_turn(last, chans).astype(BF)
    last = last.astype(BF)
    direct = jnp.concatenate([re, im, last], axis=1)
    turned = jnp.concatenate([-im, re, turned_last], axis=1)
    rows = dot(back_cos, direct) + dot(back_sin, turned)
    summed = dot(total, tail)
    summed = summed + pltpu.roll(summed, LANES - chans, 1)
    summed = jnp.where(group == 2, summed, 0.0)
    summed = summed + pltpu.roll(summed, chans, 1)
    re, im, last = lane_blocks(rows)
    out_ref[...] = pack([re, im, last + halves(summed, chans)])


def columns_back_kernel(in_ref, mixed_ref, first_ref, long_ref, out_ref, bypass_ref, *, factor):
    rows, cols, width = out_ref.shape
    chans = bypass_ref.shape[0]
    blocks = unpack(in_ref[...], 3)
    lanes = jnp.concatenate(blocks, axis=1)
    height = lanes.shape[1]
    steps = dot(lanes, long_ref[:height]).astype(BF)
    stacked = jnp.concatenate([steps[:, :width], steps[:, width:]], axis=0)
    total = dot(long_ref[height:], stacked) + mixed_ref[...]
    out_ref[...] = total.reshape(rows, cols, width).astype(BF)
    sums = dot(first_ref[...], blocks[2])
    sums = pltpu.roll(sums + pltpu.roll(sums, LANES - chans, 1), LANES // 2, 1)
    bypass_ref[...] = sums[:, :chans] * factor


def local(inputs, preactivation, cotangent, spectral, bypass):
    rows, cols, width = inputs.shape
    chans = bypass.shape[0]
    steps = width // chans
    kept, col_modes, time_modes, wide = spectral.shape[1:]
    parts = lax.axis_size("row")
    pair = col_modes // parts
    fits = (
        lax.axis_size("col") == 1
        and col_modes % parts == 0
        and pair * rows == SUB
        and pair * kept == SUB
        and parts == chans
        and 4 * chans == LANES
        and time_modes == 5
        and steps == 8
        and cols % LANES == 0
    )
    if not fits:
        return general_local(inputs, preactivation, cotangent, spectral, bypass)
    row_modes = kept * parts
    total_x = rows * parts
    factor = 1.0 / math.sqrt(float(total_x * cols * steps * row_modes * col_modes * time_modes))
    bypass_factor = 1.0 / math.sqrt(float(total_x * cols * steps))
    tables = build_tables(parts, rows, cols, steps, chans, row_modes, pair, kept, col_modes, time_modes)
    stack_all = lambda arrays: jnp.asarray(np.concatenate(arrays, axis=0))
    stack = lambda *names: stack_all([tables[name] for name in names])
    square = stack("row_cos", "row_sin")
    mixing = stack_all(
        [tables["order"], tables["unorder"]] + np.split(tables["tile"], 2, axis=1) + [tables["tile_last"]]
    )
    back_table = stack("back_cos", "back_sin", "total")
    long = stack("time_back", "col_back")
    time_table, col_table, repeat, sums, spread, place, first = [
        jnp.asarray(tables[name])
        for name in ("time", "col", "repeat", "sums", "spread_chan", "place", "first")
    ]

    def swap_parts(array):
        return lax.all_to_all(array, "row", 0, 0, tiled=True)

    like = lambda array: jax.ShapeDtypeStruct(array.shape, array.dtype)
    shape = jax.ShapeDtypeStruct
    chunk = parts * SUB
    field = (rows * cols, width)
    sent, pre_grad, square = call(
        lambda *refs: columns_kernel(*refs, chans=chans),
        (shape((5 * chunk, LANES), BF), shape(field, BF))
        + (like(square),),
        inputs, preactivation, cotangent, time_table, col_table, square,
        far=range(6),
        scratch=[pltpu.VMEM(a.shape, a.dtype) for a in (inputs, inputs, inputs, time_table, col_table)]
        + [pltpu.SemaphoreType.DMA((6,))],
    )
    weight = spectral.transpose(0, 1, 3, 2, 4)
    sent = call(
        lambda *refs: rows_kernel(*refs, chans=chans),
        shape((5 * chunk, LANES), BF),
        swap_parts(sent), square, weight,
        far=(2,),
    )
    sent, modes, repeat, back_table = call(
        lambda *refs: back_kernel(*refs, factor=factor),
        (shape((3 * chunk, LANES), BF), shape((kept * col_modes, 5 * LANES), BF), like(repeat), like(back_table)),
        swap_parts(sent), pre_grad, weight, inputs, mixing, sums, place, repeat, back_table,
        far=(7, 8),
        scratch=[pltpu.SemaphoreType.DMA((2,))],
    )
    near = pl.BlockSpec(memory_space=pltpu.VMEM)
    slots = 3
    grad_spectral = pl.pallas_call(
        lambda *refs: weight_kernel(*refs, factor=factor),
        out_shape=shape((2, kept, time_modes, col_modes, wide), jnp.float32),
        in_specs=[near, near, near],
        out_specs=pl.BlockSpec(memory_space=pltpu.HBM),
        scratch_shapes=[
            pltpu.VMEM((slots, 2, kept, col_modes, wide), jnp.float32), pltpu.SemaphoreType.DMA((slots,)),
        ],
        compiler_params=pltpu.CompilerParams(vmem_limit_bytes=16 * 1024 * 1024),
    )(*[pltpu.with_memory_space_constraint(a, pltpu.VMEM) for a in (modes, repeat, mixing)]).transpose(0, 1, 3, 2, 4)
    sent = call(
        lambda *refs: rows_back_kernel(*refs, chans=chans),
        shape((3 * chunk, LANES), BF),
        swap_parts(sent), back_table,
    )
    mixed, long, first = call(
        mixing_kernel,
        (shape(field, jnp.float32), like(long), like(first)),
        sent, pre_grad, long, first, bypass, spread,
        far=(0, 1, 2, 3),
        scratch=[pltpu.VMEM(field, BF), pltpu.SemaphoreType.DMA((3,))],
    )
    grad_inputs, grad_bypass = call(
        lambda *refs: columns_back_kernel(*refs, factor=bypass_factor),
        (shape((rows, cols, width), BF), shape((chans, chans), jnp.float32)),
        swap_parts(sent), mixed, first, long,
        keep=False,
    )
    return (grad_inputs, grad_spectral, grad_bypass)


def solution(mesh):
    return jax.shard_map(
        local,
        mesh=mesh,
        in_specs=(
            P("row", "col", None),
            P("row", "col", None),
            P("row", "col", None),
            P(None, "row", "col", None, None),
            P(),
        ),
        out_specs=(P("row", "col", None), P(None, "row", "col", None, None), P()),
        check_vma=False,
    )
```

```python
import math

import jax
import jax.numpy as jnp
import numpy as np
from jax import lax
from jax.experimental import pallas as pl
from jax.experimental.pallas import tpu as pltpu
from jax.sharding import PartitionSpec as P

exact_mode = lax.Precision.HIGHEST


def counting(length):
    return jnp.arange(length, dtype=jnp.int32)


def kept_freq(slot_index, keep_count):
    return jnp.where(slot_index < keep_count // 2, slot_index, slot_index - keep_count)


def phase_table(outer_index, inner_index, length, direction):
    turn_count = jnp.mod(outer_index[:, None] * inner_index[None, :], length)
    angles = turn_count.astype(jnp.float32) * (2.0 * math.pi / length)
    cosine = jnp.cos(angles)
    sine_part = direction * jnp.sin(angles)
    top_rows = jnp.stack([cosine, -sine_part], axis=1)
    low_rows = jnp.stack([sine_part, cosine], axis=1)
    return jnp.stack([top_rows, low_rows], axis=0)


def time_forward(step_count, time_modes):
    turn_count = jnp.mod(counting(step_count)[:, None] * counting(time_modes)[None, :], step_count)
    angles = turn_count.astype(jnp.float32) * (2.0 * math.pi / step_count)
    return jnp.stack([jnp.cos(angles), -jnp.sin(angles)], axis=1)


def time_inverse(step_count, time_modes):
    turn_count = jnp.mod(counting(time_modes)[:, None] * counting(step_count)[None, :], step_count)
    angles = turn_count.astype(jnp.float32) * (2.0 * math.pi / step_count)
    return jnp.stack([jnp.cos(angles), -jnp.sin(angles)], axis=0)


def gelu_slope(values):
    normal_cdf = 0.5 * (1.0 + lax.erf(values * (1.0 / math.sqrt(2.0))))
    density = jnp.exp(-0.5 * values * values) * (1.0 / math.sqrt(2.0 * math.pi))
    return normal_cdf + values * density


def mix_modes(modes_in, modes_grad, weight, factor):
    in_real = modes_in[:, 0]
    in_imag = modes_in[:, 1]
    grad_real = modes_grad[:, 0]
    grad_imag = modes_grad[:, 1]
    real_part = factor * (
        in_real[..., :, None] * grad_real[..., None, :]
        + in_imag[..., :, None] * grad_imag[..., None, :]
    )
    imag_part = factor * (
        in_real[..., :, None] * grad_imag[..., None, :]
        - in_imag[..., :, None] * grad_real[..., None, :]
    )
    weight_grad = jnp.stack([real_part, imag_part], axis=0)
    w_real = weight[0]
    w_imag = weight[1]
    back_real = factor * (
        jnp.einsum("kyscd,kysd->kysc", w_real, grad_real, precision=exact_mode)
        + jnp.einsum("kyscd,kysd->kysc", w_imag, grad_imag, precision=exact_mode)
    )
    back_imag = factor * (
        jnp.einsum("kyscd,kysd->kysc", w_real, grad_imag, precision=exact_mode)
        - jnp.einsum("kyscd,kysd->kysc", w_imag, grad_real, precision=exact_mode)
    )
    return (weight_grad, jnp.stack([back_real, back_imag], axis=1))


def general_local(inputs, preactivation, cotangent, spectral, bypass):
    row_count, col_count, packed = inputs.shape
    chan_count = bypass.shape[0]
    step_count = packed // chan_count
    time_modes = spectral.shape[3]
    owned_row_modes = spectral.shape[1]
    owned_col_modes = spectral.shape[2]
    row_parts = lax.axis_size("row")
    col_parts = lax.axis_size("col")
    row_modes = owned_row_modes * row_parts
    col_modes = owned_col_modes * col_parts
    total_x = row_count * row_parts
    total_y = col_count * col_parts
    factor = 1.0 / math.sqrt(
        float(total_x * total_y * step_count * row_modes * col_modes * time_modes)
    )
    row_start = lax.axis_index("row") * row_count
    col_start = lax.axis_index("col") * col_count
    mode_width = owned_col_modes * time_modes * chan_count
    slopes = gelu_slope(preactivation.astype(jnp.float32))
    pre_grad = (cotangent.astype(jnp.float32) * slopes).astype(jnp.bfloat16)
    flat_inputs = inputs.reshape(-1, chan_count)
    flat_grad = pre_grad.reshape(-1, chan_count)
    local_bypass = jnp.einsum(
        "nc,nd->cd", flat_inputs, flat_grad, preferred_element_type=jnp.float32
    )
    bypass_total = lax.psum(local_bypass, ("row", "col"))
    grad_bypass = bypass_total * (1.0 / math.sqrt(float(total_x * total_y * step_count)))
    forward_t = time_forward(step_count, time_modes)
    col_table = phase_table(counting(col_modes), col_start + counting(col_count), total_y, -1.0)

    def column_terms(field):
        cube_view = field.astype(jnp.float32).reshape(row_count, col_count, step_count, chan_count)
        in_time = jnp.einsum("rytc,tqs->ryqsc", cube_view, forward_t, precision=exact_mode)
        return jnp.einsum("akpy,rypsc->raksc", col_table, in_time, precision=exact_mode)

    col_in, col_grad = (
        lax.psum_scatter(
            column_terms(inputs).astype(jnp.bfloat16), "col", scatter_dimension=2, tiled=True
        ).astype(jnp.float32),
        lax.psum_scatter(
            column_terms(pre_grad).astype(jnp.bfloat16), "col", scatter_dimension=2, tiled=True
        ).astype(jnp.float32),
    )
    flat_in = col_in.reshape(row_count, 2, mode_width)
    flat_cols = col_grad.reshape(row_count, 2, mode_width)
    stacked = jnp.stack([flat_in, flat_cols], axis=2)
    frequencies = kept_freq(counting(owned_row_modes * lax.axis_size("row")), row_modes)
    phases = phase_table(frequencies, row_start + counting(row_count), total_x, -1.0)
    owned_modes = lax.psum_scatter(
        jnp.einsum("akpr,rpbm->kabm", phases, stacked, precision=exact_mode),
        "row",
        scatter_dimension=0,
        tiled=True,
    )
    modes_in = owned_modes[:, :, 0]
    modes_grad = owned_modes[:, :, 1]
    mode_shape = (owned_row_modes, 2, owned_col_modes, time_modes, chan_count)
    weight = spectral.astype(jnp.float32).reshape(
        2, owned_row_modes, owned_col_modes, time_modes, chan_count, chan_count
    )
    weight_grad, back_modes = mix_modes(
        modes_in.reshape(mode_shape), modes_grad.reshape(mode_shape), weight, factor
    )
    grad_spectral = weight_grad.reshape(spectral.shape)
    flat_back = back_modes.reshape(owned_row_modes, 2, mode_width)
    mode_piece = lax.all_gather(flat_back, "row", axis=0, tiled=True)
    span_count = mode_piece.shape[0]
    frequencies = kept_freq(counting(span_count), row_modes)
    phases = phase_table(row_start + counting(row_count), frequencies, total_x, 1.0)
    rows_back = jnp.einsum("axpk,kpm->xam", phases, mode_piece, precision=exact_mode)
    rows_view = rows_back.reshape(row_count, 2, owned_col_modes, time_modes, chan_count)
    col_piece = lax.all_gather(rows_view.astype(jnp.bfloat16), "col", axis=2, tiled=True).astype(
        jnp.float32
    )
    span_count = col_piece.shape[2]
    phases = phase_table(col_start + counting(col_count), counting(span_count), total_y, 1.0)
    cells_y = jnp.zeros(
        (row_count, col_count, 2, time_modes, chan_count), jnp.float32
    ) + jnp.einsum("aypk,rpksc->ryasc", phases, col_piece, precision=exact_mode)
    kernel_grad = jnp.einsum(
        "ryasc,ast->rytc", cells_y, time_inverse(step_count, time_modes), precision=exact_mode
    )
    bypass_grad = jnp.einsum("nd,cd->nc", flat_grad, bypass, preferred_element_type=jnp.float32)
    total_grad = kernel_grad.reshape(-1, chan_count) + bypass_grad
    grad_inputs = total_grad.reshape(inputs.shape).astype(jnp.bfloat16)
    return (grad_inputs, grad_spectral, grad_bypass)


BF = jnp.bfloat16
LANES = 128
SUB = 8


def dot(a, b):
    return jnp.dot(a, b, preferred_element_type=jnp.float32)


def cos_sin(turns, length):
    angles = 2.0 * np.pi * np.mod(turns, length) / length
    return np.cos(angles), np.sin(angles)


def build_tables(parts, rows, cols, steps, chans, row_modes, pair, kept, col_modes, time_modes):
    lead = LANES // chans
    eye = np.eye(chans)
    t_index = np.arange(steps)
    tables = {}
    cos_t, sin_t = cos_sin(np.outer(t_index, np.arange(time_modes)), steps)
    real = [np.kron(cos_t[:, k : k + 1], eye) for k in range(time_modes)]
    imag = [np.kron(-sin_t[:, k : k + 1], eye) for k in range(1, lead)]
    tables["time"] = np.concatenate(real + imag, axis=1)
    ky = np.arange(col_modes)
    y = np.arange(cols)
    cos_y, sin_y = cos_sin(np.outer(ky, y), cols)
    tables["col"] = np.repeat(np.concatenate([cos_y, sin_y], axis=0), rows, axis=0)
    same_row = np.eye(rows)
    col_cos = np.einsum("ky,rs->krsy", cos_y, same_row).reshape(col_modes * rows, rows * cols)
    col_sin = np.einsum("ky,rs->krsy", sin_y, same_row).reshape(col_modes * rows, rows * cols)
    slot = np.arange(row_modes)
    freq = np.where(slot < row_modes // 2, slot, slot - row_modes)
    total_x = parts * rows
    cos_x, sin_x = cos_sin(np.outer(freq, np.arange(total_x)), total_x)
    same_pair = np.eye(pair)

    def spread(matrix):
        blocks = matrix.reshape(parts, kept, parts, rows)
        return np.einsum("ekdr,pq->epkdqr", blocks, same_pair).reshape(
            parts * pair * kept, parts * pair * rows
        )

    tables["row_cos"] = spread(cos_x)
    tables["row_sin"] = spread(sin_x)
    tables["back_cos"] = spread(cos_x).T
    tables["back_sin"] = spread(sin_x).T
    order = np.zeros((kept, col_modes, parts, pair, kept))
    for k in range(kept):
        for e in range(parts):
            for p in range(pair):
                order[k, e * pair + p, e, p, k] = 1.0
    tables["order"] = order.reshape(kept * col_modes, parts * pair * kept)
    tables["unorder"] = tables["order"].T
    wide = chans * chans
    repeat = np.kron(eye, np.ones((1, chans)))
    tiled = np.kron(np.ones((1, lead)), eye)
    group = np.zeros((lead + 1, LANES, wide))
    for k in range(lead):
        group[k, k * chans : (k + 1) * chans] = repeat
    extra = np.zeros((LANES, wide))
    extra[chans : 2 * chans] = repeat
    group[lead, :chans] = repeat
    tables["repeat"] = np.concatenate([group, extra[None]], axis=0)
    spots = np.eye(lead)
    tables["tile"] = np.concatenate([np.kron(spots[:, k : k + 1], tiled) for k in range(lead)], axis=1)
    tables["tile_last"] = np.concatenate([np.kron(spots[:, k : k + 1], tiled) for k in (2, 3)], axis=1)
    tables["sums"] = np.tile(repeat.T, (1, lead))
    re_c, re_s = np.kron(cos_t.T, eye), np.kron(sin_t.T, eye)
    cut = lead * chans
    rest = np.zeros((LANES - 2 * chans, steps * chans))
    to_cos = np.concatenate([re_c[:cut], -re_s[:cut], re_c[cut:], -re_s[cut:], rest], axis=0)
    to_sin = np.concatenate([-re_s[:cut], -re_c[:cut], -re_s[cut:], -re_c[cut:], rest], axis=0)
    tables["time_back"] = np.concatenate([to_cos, to_sin], axis=1)
    tables["col_back"] = np.concatenate([col_cos.T, col_sin.T], axis=1)
    place = np.zeros((parts, SUB, chans))
    for c in range(chans):
        place[c, :, c] = 1.0
    tables["place"] = place.reshape(parts * SUB, chans)
    pick = np.zeros((parts, SUB))
    pick[:, 0] = 1.0
    tables["total"] = np.broadcast_to(pick.reshape(1, -1), (parts * SUB, parts * SUB))
    first = np.zeros((chans, parts, SUB))
    for c in range(chans):
        first[c, c, 0] = 1.0
    tables["first"] = first.reshape(chans, parts * SUB)
    tables["spread_chan"] = np.kron(np.ones((steps, 1)), eye)
    return {name: np.asarray(table, np.float32).astype(jnp.bfloat16) for name, table in tables.items()}


def call(kernel, out_shapes, *operands, scratch=(), far=(), limit=12, keep=True, away=False):
    near = pl.BlockSpec(memory_space=pltpu.VMEM)
    stay = pl.BlockSpec(memory_space=pltpu.HBM)
    space = lambda i: pltpu.HBM if i in far else pltpu.VMEM
    operands = [pltpu.with_memory_space_constraint(a, space(i)) for i, a in enumerate(operands)]
    hold = lambda a: pltpu.VMEM(a.shape, a.dtype) if keep else a
    return pl.pallas_call(
        kernel,
        out_shape=jax.tree.map(hold, out_shapes),
        in_specs=[stay if i in far else near for i in range(len(operands))],
        out_specs=stay if away else jax.tree.map(lambda _: near, out_shapes),
        scratch_shapes=list(scratch),
        compiler_params=pltpu.CompilerParams(vmem_limit_bytes=limit * 1024 * 1024),
    )(*operands)


def lane_blocks(values):
    return [values[:, i * LANES : (i + 1) * LANES] for i in range(values.shape[1] // LANES)]


def pack(blocks):
    parts = blocks[0].shape[0] // SUB
    stacked = jnp.concatenate([b.reshape(parts, SUB, LANES) for b in blocks], axis=1)
    return stacked.reshape(-1, LANES).astype(BF)


def unpack(rows, count):
    cube = rows.astype(jnp.float32).reshape(-1, count * SUB, LANES)
    return [cube[:, i * SUB : (i + 1) * SUB].reshape(-1, LANES).astype(BF) for i in range(count)]


def lane_group(shape, chans):
    return lax.broadcasted_iota(jnp.int32, shape, 1) // chans


def halves(values, chans):
    high = values.astype(BF).astype(jnp.float32)
    group = lane_group(values.shape, chans)
    return jnp.where(group == 2, high, jnp.where(group == 3, values - high, 0.0))


def diagonal(values, chans):
    row_step = lax.broadcasted_iota(jnp.int32, values.shape, 0) // chans
    return jnp.where(row_step == lane_group(values.shape, chans), values, 0.0)


def start_copies(sems, *pairs):
    copies = [pltpu.make_async_copy(src, dst, sems.at[i]) for i, (src, dst) in enumerate(pairs)]
    for copy in copies:
        copy.start()
    return copies


def columns_kernel(
    in_hbm, pre_hbm, cot_hbm, time_hbm, col_hbm, square_hbm,
    out_ref, grad_ref, square_ref,
    in_ref, pre_ref, cot_ref, time_ref, col_ref, sems, *, chans,
):
    copies = start_copies(
        sems,
        (pre_hbm, pre_ref), (cot_hbm, cot_ref), (in_hbm, in_ref), (time_hbm, time_ref), (col_hbm, col_ref),
        (square_hbm, square_ref),
    )
    rows, cols, width = in_ref.shape
    for copy in copies[:5]:
        copy.wait()
    slopes = gelu_slope(pre_ref[...].reshape(rows * cols, width).astype(jnp.float32))
    grad = (cot_ref[...].reshape(rows * cols, width).astype(jnp.float32) * slopes).astype(BF)
    grad_ref[...] = grad
    field = in_ref[...].reshape(rows * cols, width)
    times = jnp.concatenate([dot(field, time_ref[...]), dot(grad, time_ref[...])], axis=1).astype(BF)
    col = col_ref[...]
    row = lax.broadcasted_iota(jnp.int32, col.shape, 0) % rows
    across = jnp.concatenate([jnp.where(row == r, col, jnp.zeros_like(col)) for r in range(rows)], axis=1)
    waves = dot(across, times)
    half = waves.shape[0] // 2
    in_cos, in_cos2, gr_cos, gr_cos2 = lane_blocks(waves[:half])
    in_sin, in_sin2, gr_sin, gr_sin2 = lane_blocks(waves[half:])
    alone = lane_group(in_cos.shape, chans) == 0
    last = jnp.where(alone, in_cos2, 0.0)
    for place, part in enumerate((-in_sin2, gr_cos2, -gr_sin2)):
        last = last + pltpu.roll(jnp.where(alone, part, 0.0), (place + 1) * chans, 1)
    out_ref[...] = pack(
        [
            in_cos + jnp.where(alone, 0.0, in_sin2),
            jnp.where(alone, 0.0, in_cos2) - in_sin,
            gr_cos + jnp.where(alone, 0.0, gr_sin2),
            jnp.where(alone, 0.0, gr_cos2) - gr_sin,
            last,
        ]
    )
    for copy in copies[5:]:
        copy.wait()


def bypass_terms(field, grad, place, chans):
    products = lax.dot_general(
        field, grad, (((0,), (0,)), ((), ())), preferred_element_type=jnp.float32
    )
    products = diagonal(products, chans)
    partial = products[:chans]
    for step in range(1, field.shape[1] // chans):
        partial = partial + products[step * chans : (step + 1) * chans]
    folded = sum(lane_blocks(partial))
    shift = LANES // 2
    while shift >= chans:
        folded = folded + pltpu.roll(folded, shift, 1)
        shift //= 2
    return dot(place, halves(folded, chans).astype(BF))


def mixing_kernel(
    sent_hbm, grad_hbm, long_hbm, first_hbm, bypass_ref, spread_ref, mixed_ref, long_ref, first_ref, grad_ref, sems
):
    del sent_hbm
    copies = start_copies(sems, (grad_hbm, grad_ref), (long_hbm, long_ref), (first_hbm, first_ref))
    chans = bypass_ref.shape[0]
    spread = spread_ref[...]
    across = lax.dot_general(
        bypass_ref[...], spread, (((0,), (1,)), ((), ())), preferred_element_type=jnp.float32
    ).astype(BF)
    matrix = diagonal(dot(spread, across), chans).astype(BF)
    copies[0].wait()
    mixed_ref[...] = dot(grad_ref[...], matrix)
    for copy in copies[1:]:
        copy.wait()


def quarter_turn(values, chans):
    ahead, behind = pltpu.roll(values, LANES - chans, 1), pltpu.roll(values, chans, 1)
    return jnp.where(lane_group(values.shape, chans) % 2 == 0, ahead, -behind)


def rows_kernel(in_ref, square_ref, weight_hbm, out_ref, *, chans):
    del weight_hbm
    in_re, in_im, gr_re, gr_im, last = unpack(in_ref[...], 5)
    size = square_ref.shape[1]
    turned_last = quarter_turn(last.astype(jnp.float32), chans).astype(BF)
    direct = jnp.concatenate([in_re, in_im, gr_re, gr_im, last], axis=1)
    turned = jnp.concatenate([in_im, -in_re, gr_im, -gr_re, turned_last], axis=1)
    modes = dot(square_ref[:size], direct) + dot(square_ref[size : 2 * size], turned)
    out_ref[...] = pack(lane_blocks(modes))


def mixing_tables(table_ref):
    size = table_ref.shape[1]
    tiles = [table_ref[2 * size + i * LANES : 2 * size + (i + 1) * LANES] for i in range(3)]
    return table_ref[:size], table_ref[size : 2 * size], *tiles


def back_kernel(
    in_ref, grad_ref, weight_ref, field_ref, table_ref, sums_ref, place_ref, repeat_hbm, rows_hbm,
    out_ref, modes_ref, repeat_ref, rows_ref, sems, *, factor,
):
    chans = place_ref.shape[1]
    copies = start_copies(sems, (rows_hbm, rows_ref), (repeat_hbm, repeat_ref))
    size = table_ref.shape[1]
    order, unorder, tile_a, tile_b, tile_last = mixing_tables(table_ref)
    lanes = jnp.concatenate(unpack(in_ref[...], 5), axis=1)
    modes = dot(order, lanes).astype(BF)
    modes_ref[...] = modes
    steps = weight_ref.shape[2]
    wide = weight_ref.shape[4]
    lead = LANES // chans
    gr_re, gr_im, last = lane_blocks(modes)[2:]
    first = jnp.concatenate([gr_re, gr_im], axis=1)
    blank = jnp.zeros((LANES, LANES), BF)
    tiles = [
        jnp.concatenate([jnp.concatenate([t, blank], axis=1), jnp.concatenate([blank, t], axis=1)], axis=0)
        for t in lane_blocks(tile_a) + lane_blocks(tile_b)
    ]
    group = lane_group((size, LANES), chans)
    re_sum = im_sum = jnp.zeros((size, LANES), jnp.float32)
    for k in range(steps):
        g_re, g_im = lane_blocks((dot(first, tiles[k]) if k < lead else dot(last, tile_last)).astype(BF))
        p_re, p_im = [], []
        for j in range(wide // LANES):
            w_re = weight_ref[0, :, k, :, j * LANES : (j + 1) * LANES].reshape(size, LANES)
            w_im = weight_ref[1, :, k, :, j * LANES : (j + 1) * LANES].reshape(size, LANES)
            p_re.append(w_re * g_re + w_im * g_im)
            p_im.append(w_re * g_im - w_im * g_re)
        both = jnp.concatenate([jnp.concatenate(p_re, axis=1), jnp.concatenate(p_im, axis=1)], axis=0)
        summed = dot(both, sums_ref[...])
        if k < lead:
            re_sum = jnp.where(group == k, summed[:size], re_sum)
            im_sum = jnp.where(group == k, summed[size:], im_sum)
        else:
            last_sum = jnp.where(group == 0, summed[:size], jnp.where(group == 1, summed[size:], 0.0))
    rows, cols, width = field_ref.shape
    terms = bypass_terms(field_ref[...].reshape(rows * cols, width), grad_ref[...], place_ref[...], chans)
    back = (jnp.concatenate([re_sum, im_sum, last_sum], axis=1) * factor).astype(BF)
    re, im, last = lane_blocks(dot(unorder, back))
    out_ref[...] = pack([re, im, last + terms])
    for copy in copies:
        copy.wait()


def weight_kernel(modes_ref, repeat_ref, table_ref, out_hbm, out_ref, sems, *, factor):
    slots, _, kept, count, wide = out_ref.shape
    steps = out_hbm.shape[2]
    lead = repeat_ref.shape[0] - 2
    in_re, in_im, gr_re, gr_im, last = lane_blocks(modes_ref[...])
    _, _, tile_a, tile_b, tile_last = mixing_tables(table_ref)
    tiled = [lane_blocks(dot(g, tile_a) * factor) + lane_blocks(dot(g, tile_b) * factor) for g in (gr_re, gr_im)]
    tiled = list(zip(*tiled)) + [lane_blocks(dot(last, tile_last) * factor)]
    copies = []
    for k in range(steps):
        if k < lead:
            a_re, a_im = dot(in_re, repeat_ref[k]), dot(in_im, repeat_ref[k])
        else:
            a_re, a_im = dot(last, repeat_ref[lead]), dot(last, repeat_ref[lead + 1])
        b_re, b_im = tiled[k]
        slot = k % slots
        if k >= slots:
            copies[k - slots].wait()
        for j in range(wide // LANES):
            part = slice(j * LANES, (j + 1) * LANES)
            out_ref[slot, 0, :, :, part] = (a_re[:, part] * b_re + a_im[:, part] * b_im).reshape(kept, count, LANES)
            out_ref[slot, 1, :, :, part] = (a_re[:, part] * b_im - a_im[:, part] * b_re).reshape(kept, count, LANES)
        copies.append(pltpu.make_async_copy(out_ref.at[slot], out_hbm.at[:, :, k], sems.at[slot]))
        copies[k].start()
    for copy in copies[max(0, steps - slots) :]:
        copy.wait()


def rows_back_kernel(in_ref, table_ref, out_hbm, out_ref, sems, *, chans):
    re, im, tail = unpack(in_ref[...], 3)
    size = table_ref.shape[1]
    back_cos, back_sin, total = [table_ref[i * size : (i + 1) * size] for i in range(3)]
    group = lane_group(tail.shape, chans)
    last = jnp.where(group < 2, tail.astype(jnp.float32), 0.0)
    turned_last = -quarter_turn(last, chans).astype(BF)
    last = last.astype(BF)
    direct = jnp.concatenate([re, im, last], axis=1)
    turned = jnp.concatenate([-im, re, turned_last], axis=1)
    summed = dot(total, tail)
    summed = summed + pltpu.roll(summed, LANES - chans, 1)
    summed = jnp.where(group == 2, summed, 0.0)
    terms = halves(summed + pltpu.roll(summed, chans, 1), chans)
    copies = []
    pieces = sems.shape[0]
    step, long = size // pieces, out_ref.shape[0] // pieces
    for i in range(pieces):
        here, there = slice(i * step, (i + 1) * step), slice(i * long, (i + 1) * long)
        rows = dot(back_cos[here], direct) + dot(back_sin[here], turned)
        re, im, last = lane_blocks(rows)
        out_ref[there] = pack([re, im, last + terms[here]])
        copies.append(pltpu.make_async_copy(out_ref.at[there], out_hbm.at[there], sems.at[i]))
        copies[i].start()
    for copy in copies:
        copy.wait()


def columns_back_kernel(in_ref, mixed_ref, first_ref, long_ref, out_ref, bypass_ref, *, factor):
    rows, cols, width = out_ref.shape
    chans = bypass_ref.shape[0]
    blocks = unpack(in_ref[...], 3)
    lanes = jnp.concatenate(blocks, axis=1)
    height = lanes.shape[1]
    steps = dot(lanes, long_ref[:height]).astype(BF)
    stacked = jnp.concatenate([steps[:, :width], steps[:, width:]], axis=0)
    total = dot(long_ref[height:], stacked) + mixed_ref[...]
    out_ref[...] = total.reshape(rows, cols, width).astype(BF)
    sums = dot(first_ref[...], blocks[2])
    sums = pltpu.roll(sums + pltpu.roll(sums, LANES - chans, 1), LANES // 2, 1)
    bypass_ref[...] = sums[:, :chans] * factor


def local(inputs, preactivation, cotangent, spectral, bypass):
    rows, cols, width = inputs.shape
    chans = bypass.shape[0]
    steps = width // chans
    kept, col_modes, time_modes, wide = spectral.shape[1:]
    parts = lax.axis_size("row")
    pair = col_modes // parts
    fits = (
        lax.axis_size("col") == 1
        and col_modes % parts == 0
        and pair * rows == SUB
        and pair * kept == SUB
        and parts == chans
        and 4 * chans == LANES
        and time_modes == 5
        and steps == 8
        and cols % LANES == 0
    )
    if not fits:
        return general_local(inputs, preactivation, cotangent, spectral, bypass)
    row_modes = kept * parts
    total_x = rows * parts
    factor = 1.0 / math.sqrt(float(total_x * cols * steps * row_modes * col_modes * time_modes))
    bypass_factor = 1.0 / math.sqrt(float(total_x * cols * steps))
    tables = build_tables(parts, rows, cols, steps, chans, row_modes, pair, kept, col_modes, time_modes)
    stack_all = lambda arrays: jnp.asarray(np.concatenate(arrays, axis=0))
    stack = lambda *names: stack_all([tables[name] for name in names])
    square = stack("row_cos", "row_sin")
    mixing = stack_all(
        [tables["order"], tables["unorder"]] + np.split(tables["tile"], 2, axis=1) + [tables["tile_last"]]
    )
    back_table = stack("back_cos", "back_sin", "total")
    long = stack("time_back", "col_back")
    time_table, col_table, repeat, sums, spread, place, first = [
        jnp.asarray(tables[name])
        for name in ("time", "col", "repeat", "sums", "spread_chan", "place", "first")
    ]

    def swap_parts(array):
        return lax.all_to_all(array, "row", 0, 0, tiled=True)

    like = lambda array: jax.ShapeDtypeStruct(array.shape, array.dtype)
    shape = jax.ShapeDtypeStruct
    chunk = parts * SUB
    field = (rows * cols, width)
    sent, pre_grad, square = call(
        lambda *refs: columns_kernel(*refs, chans=chans),
        (shape((5 * chunk, LANES), BF), shape(field, BF))
        + (like(square),),
        inputs, preactivation, cotangent, time_table, col_table, square,
        far=range(6),
        scratch=[pltpu.VMEM(a.shape, a.dtype) for a in (inputs, inputs, inputs, time_table, col_table)]
        + [pltpu.SemaphoreType.DMA((6,))],
    )
    weight = spectral.transpose(0, 1, 3, 2, 4)
    sent = call(
        lambda *refs: rows_kernel(*refs, chans=chans),
        shape((5 * chunk, LANES), BF),
        swap_parts(sent), square, weight,
        far=(2,),
    )
    sent, modes, repeat, back_table = call(
        lambda *refs: back_kernel(*refs, factor=factor),
        (shape((3 * chunk, LANES), BF), shape((kept * col_modes, 5 * LANES), BF), like(repeat), like(back_table)),
        swap_parts(sent), pre_grad, weight, inputs, mixing, sums, place, repeat, back_table,
        far=(7, 8),
        scratch=[pltpu.SemaphoreType.DMA((2,))],
    )
    near = pl.BlockSpec(memory_space=pltpu.VMEM)
    slots = 3
    grad_spectral = pl.pallas_call(
        lambda *refs: weight_kernel(*refs, factor=factor),
        out_shape=shape((2, kept, time_modes, col_modes, wide), jnp.float32),
        in_specs=[near, near, near],
        out_specs=pl.BlockSpec(memory_space=pltpu.HBM),
        scratch_shapes=[
            pltpu.VMEM((slots, 2, kept, col_modes, wide), jnp.float32), pltpu.SemaphoreType.DMA((slots,)),
        ],
        compiler_params=pltpu.CompilerParams(vmem_limit_bytes=16 * 1024 * 1024),
    )(*[pltpu.with_memory_space_constraint(a, pltpu.VMEM) for a in (modes, repeat, mixing)]).transpose(0, 1, 3, 2, 4)
    sent = call(
        lambda *refs: rows_back_kernel(*refs, chans=chans),
        shape((3 * chunk, LANES), BF),
        swap_parts(sent), back_table,
        keep=False,
        away=True,
        scratch=[pltpu.VMEM((3 * chunk, LANES), BF), pltpu.SemaphoreType.DMA((2,))],
    )
    mixed, long, first = call(
        mixing_kernel,
        (shape(field, jnp.float32), like(long), like(first)),
        sent, pre_grad, long, first, bypass, spread,
        far=(0, 1, 2, 3),
        scratch=[pltpu.VMEM(field, BF), pltpu.SemaphoreType.DMA((3,))],
    )
    grad_inputs, grad_bypass = call(
        lambda *refs: columns_back_kernel(*refs, factor=bypass_factor),
        (shape((rows, cols, width), BF), shape((chans, chans), jnp.float32)),
        swap_parts(sent), mixed, first, long,
        keep=False,
    )
    return (grad_inputs, grad_spectral, grad_bypass)


def solution(mesh):
    return jax.shard_map(
        local,
        mesh=mesh,
        in_specs=(
            P("row", "col", None),
            P("row", "col", None),
            P("row", "col", None),
            P(None, "row", "col", None, None),
            P(),
        ),
        out_specs=(P("row", "col", None), P(None, "row", "col", None, None), P()),
        check_vma=False,
    )
```

```python
import math

import jax
import jax.numpy as jnp
import numpy as np
from jax import lax
from jax.experimental import pallas as pl
from jax.experimental.pallas import tpu as pltpu
from jax.sharding import PartitionSpec as P

exact_mode = lax.Precision.HIGHEST


def counting(length):
    return jnp.arange(length, dtype=jnp.int32)


def kept_freq(slot_index, keep_count):
    return jnp.where(slot_index < keep_count // 2, slot_index, slot_index - keep_count)


def phase_table(outer_index, inner_index, length, direction):
    turn_count = jnp.mod(outer_index[:, None] * inner_index[None, :], length)
    angles = turn_count.astype(jnp.float32) * (2.0 * math.pi / length)
    cosine = jnp.cos(angles)
    sine_part = direction * jnp.sin(angles)
    top_rows = jnp.stack([cosine, -sine_part], axis=1)
    low_rows = jnp.stack([sine_part, cosine], axis=1)
    return jnp.stack([top_rows, low_rows], axis=0)


def time_forward(step_count, time_modes):
    turn_count = jnp.mod(counting(step_count)[:, None] * counting(time_modes)[None, :], step_count)
    angles = turn_count.astype(jnp.float32) * (2.0 * math.pi / step_count)
    return jnp.stack([jnp.cos(angles), -jnp.sin(angles)], axis=1)


def time_inverse(step_count, time_modes):
    turn_count = jnp.mod(counting(time_modes)[:, None] * counting(step_count)[None, :], step_count)
    angles = turn_count.astype(jnp.float32) * (2.0 * math.pi / step_count)
    return jnp.stack([jnp.cos(angles), -jnp.sin(angles)], axis=0)


def gelu_slope(values):
    normal_cdf = 0.5 * (1.0 + lax.erf(values * (1.0 / math.sqrt(2.0))))
    density = jnp.exp(-0.5 * values * values) * (1.0 / math.sqrt(2.0 * math.pi))
    return normal_cdf + values * density


def mix_modes(modes_in, modes_grad, weight, factor):
    in_real = modes_in[:, 0]
    in_imag = modes_in[:, 1]
    grad_real = modes_grad[:, 0]
    grad_imag = modes_grad[:, 1]
    real_part = factor * (
        in_real[..., :, None] * grad_real[..., None, :]
        + in_imag[..., :, None] * grad_imag[..., None, :]
    )
    imag_part = factor * (
        in_real[..., :, None] * grad_imag[..., None, :]
        - in_imag[..., :, None] * grad_real[..., None, :]
    )
    weight_grad = jnp.stack([real_part, imag_part], axis=0)
    w_real = weight[0]
    w_imag = weight[1]
    back_real = factor * (
        jnp.einsum("kyscd,kysd->kysc", w_real, grad_real, precision=exact_mode)
        + jnp.einsum("kyscd,kysd->kysc", w_imag, grad_imag, precision=exact_mode)
    )
    back_imag = factor * (
        jnp.einsum("kyscd,kysd->kysc", w_real, grad_imag, precision=exact_mode)
        - jnp.einsum("kyscd,kysd->kysc", w_imag, grad_real, precision=exact_mode)
    )
    return (weight_grad, jnp.stack([back_real, back_imag], axis=1))


def general_local(inputs, preactivation, cotangent, spectral, bypass):
    row_count, col_count, packed = inputs.shape
    chan_count = bypass.shape[0]
    step_count = packed // chan_count
    time_modes = spectral.shape[3]
    owned_row_modes = spectral.shape[1]
    owned_col_modes = spectral.shape[2]
    row_parts = lax.axis_size("row")
    col_parts = lax.axis_size("col")
    row_modes = owned_row_modes * row_parts
    col_modes = owned_col_modes * col_parts
    total_x = row_count * row_parts
    total_y = col_count * col_parts
    factor = 1.0 / math.sqrt(
        float(total_x * total_y * step_count * row_modes * col_modes * time_modes)
    )
    row_start = lax.axis_index("row") * row_count
    col_start = lax.axis_index("col") * col_count
    mode_width = owned_col_modes * time_modes * chan_count
    slopes = gelu_slope(preactivation.astype(jnp.float32))
    pre_grad = (cotangent.astype(jnp.float32) * slopes).astype(jnp.bfloat16)
    flat_inputs = inputs.reshape(-1, chan_count)
    flat_grad = pre_grad.reshape(-1, chan_count)
    local_bypass = jnp.einsum(
        "nc,nd->cd", flat_inputs, flat_grad, preferred_element_type=jnp.float32
    )
    bypass_total = lax.psum(local_bypass, ("row", "col"))
    grad_bypass = bypass_total * (1.0 / math.sqrt(float(total_x * total_y * step_count)))
    forward_t = time_forward(step_count, time_modes)
    col_table = phase_table(counting(col_modes), col_start + counting(col_count), total_y, -1.0)

    def column_terms(field):
        cube_view = field.astype(jnp.float32).reshape(row_count, col_count, step_count, chan_count)
        in_time = jnp.einsum("rytc,tqs->ryqsc", cube_view, forward_t, precision=exact_mode)
        return jnp.einsum("akpy,rypsc->raksc", col_table, in_time, precision=exact_mode)

    col_in, col_grad = (
        lax.psum_scatter(
            column_terms(inputs).astype(jnp.bfloat16), "col", scatter_dimension=2, tiled=True
        ).astype(jnp.float32),
        lax.psum_scatter(
            column_terms(pre_grad).astype(jnp.bfloat16), "col", scatter_dimension=2, tiled=True
        ).astype(jnp.float32),
    )
    flat_in = col_in.reshape(row_count, 2, mode_width)
    flat_cols = col_grad.reshape(row_count, 2, mode_width)
    stacked = jnp.stack([flat_in, flat_cols], axis=2)
    frequencies = kept_freq(counting(owned_row_modes * lax.axis_size("row")), row_modes)
    phases = phase_table(frequencies, row_start + counting(row_count), total_x, -1.0)
    owned_modes = lax.psum_scatter(
        jnp.einsum("akpr,rpbm->kabm", phases, stacked, precision=exact_mode),
        "row",
        scatter_dimension=0,
        tiled=True,
    )
    modes_in = owned_modes[:, :, 0]
    modes_grad = owned_modes[:, :, 1]
    mode_shape = (owned_row_modes, 2, owned_col_modes, time_modes, chan_count)
    weight = spectral.astype(jnp.float32).reshape(
        2, owned_row_modes, owned_col_modes, time_modes, chan_count, chan_count
    )
    weight_grad, back_modes = mix_modes(
        modes_in.reshape(mode_shape), modes_grad.reshape(mode_shape), weight, factor
    )
    grad_spectral = weight_grad.reshape(spectral.shape)
    flat_back = back_modes.reshape(owned_row_modes, 2, mode_width)
    mode_piece = lax.all_gather(flat_back, "row", axis=0, tiled=True)
    span_count = mode_piece.shape[0]
    frequencies = kept_freq(counting(span_count), row_modes)
    phases = phase_table(row_start + counting(row_count), frequencies, total_x, 1.0)
    rows_back = jnp.einsum("axpk,kpm->xam", phases, mode_piece, precision=exact_mode)
    rows_view = rows_back.reshape(row_count, 2, owned_col_modes, time_modes, chan_count)
    col_piece = lax.all_gather(rows_view.astype(jnp.bfloat16), "col", axis=2, tiled=True).astype(
        jnp.float32
    )
    span_count = col_piece.shape[2]
    phases = phase_table(col_start + counting(col_count), counting(span_count), total_y, 1.0)
    cells_y = jnp.zeros(
        (row_count, col_count, 2, time_modes, chan_count), jnp.float32
    ) + jnp.einsum("aypk,rpksc->ryasc", phases, col_piece, precision=exact_mode)
    kernel_grad = jnp.einsum(
        "ryasc,ast->rytc", cells_y, time_inverse(step_count, time_modes), precision=exact_mode
    )
    bypass_grad = jnp.einsum("nd,cd->nc", flat_grad, bypass, preferred_element_type=jnp.float32)
    total_grad = kernel_grad.reshape(-1, chan_count) + bypass_grad
    grad_inputs = total_grad.reshape(inputs.shape).astype(jnp.bfloat16)
    return (grad_inputs, grad_spectral, grad_bypass)


BF = jnp.bfloat16
LANES = 128
SUB = 8


def dot(a, b):
    return jnp.dot(a, b, preferred_element_type=jnp.float32)


def cos_sin(turns, length):
    angles = 2.0 * np.pi * np.mod(turns, length) / length
    return np.cos(angles), np.sin(angles)


def build_tables(parts, rows, cols, steps, chans, row_modes, pair, kept, col_modes, time_modes):
    lead = LANES // chans
    eye = np.eye(chans)
    t_index = np.arange(steps)
    tables = {}
    cos_t, sin_t = cos_sin(np.outer(t_index, np.arange(time_modes)), steps)
    real = [np.kron(cos_t[:, k : k + 1], eye) for k in range(time_modes)]
    imag = [np.kron(-sin_t[:, k : k + 1], eye) for k in range(1, lead)]
    tables["time"] = np.concatenate(real + imag, axis=1)
    ky = np.arange(col_modes)
    y = np.arange(cols)
    cos_y, sin_y = cos_sin(np.outer(ky, y), cols)
    tables["col"] = np.repeat(np.concatenate([cos_y, sin_y], axis=0), rows, axis=0)
    same_row = np.eye(rows)
    col_cos = np.einsum("ky,rs->krsy", cos_y, same_row).reshape(col_modes * rows, rows * cols)
    col_sin = np.einsum("ky,rs->krsy", sin_y, same_row).reshape(col_modes * rows, rows * cols)
    slot = np.arange(row_modes)
    freq = np.where(slot < row_modes // 2, slot, slot - row_modes)
    total_x = parts * rows
    cos_x, sin_x = cos_sin(np.outer(freq, np.arange(total_x)), total_x)
    same_pair = np.eye(pair)

    def spread(matrix):
        blocks = matrix.reshape(parts, kept, parts, rows)
        return np.einsum("ekdr,pq->epkdqr", blocks, same_pair).reshape(
            parts * pair * kept, parts * pair * rows
        )

    tables["row_cos"] = spread(cos_x)
    tables["row_sin"] = spread(sin_x)
    tables["back_cos"] = spread(cos_x).T
    tables["back_sin"] = spread(sin_x).T
    order = np.zeros((kept, col_modes, parts, pair, kept))
    for k in range(kept):
        for e in range(parts):
            for p in range(pair):
                order[k, e * pair + p, e, p, k] = 1.0
    tables["order"] = order.reshape(kept * col_modes, parts * pair * kept)
    tables["unorder"] = tables["order"].T
    wide = chans * chans
    repeat = np.kron(eye, np.ones((1, chans)))
    tiled = np.kron(np.ones((1, lead)), eye)
    group = np.zeros((lead + 1, LANES, wide))
    for k in range(lead):
        group[k, k * chans : (k + 1) * chans] = repeat
    extra = np.zeros((LANES, wide))
    extra[chans : 2 * chans] = repeat
    group[lead, :chans] = repeat
    tables["repeat"] = np.concatenate([group, extra[None]], axis=0)
    spots = np.eye(lead)
    tables["tile"] = np.concatenate([np.kron(spots[:, k : k + 1], tiled) for k in range(lead)], axis=1)
    tables["tile_last"] = np.concatenate([np.kron(spots[:, k : k + 1], tiled) for k in (2, 3)], axis=1)
    tables["sums"] = np.tile(repeat.T, (1, lead))
    re_c, re_s = np.kron(cos_t.T, eye), np.kron(sin_t.T, eye)
    cut = lead * chans
    rest = np.zeros((LANES - 2 * chans, steps * chans))
    to_cos = np.concatenate([re_c[:cut], -re_s[:cut], re_c[cut:], -re_s[cut:], rest], axis=0)
    to_sin = np.concatenate([-re_s[:cut], -re_c[:cut], -re_s[cut:], -re_c[cut:], rest], axis=0)
    tables["time_back"] = np.concatenate([to_cos, to_sin], axis=1)
    tables["col_back"] = np.concatenate([col_cos.T, col_sin.T], axis=1)
    place = np.zeros((parts, SUB, chans))
    for c in range(chans):
        place[c, :, c] = 1.0
    tables["place"] = place.reshape(parts * SUB, chans)
    pick = np.zeros((parts, SUB))
    pick[:, 0] = 1.0
    tables["total"] = np.broadcast_to(pick.reshape(1, -1), (parts * SUB, parts * SUB))
    first = np.zeros((chans, parts, SUB))
    for c in range(chans):
        first[c, c, 0] = 1.0
    tables["first"] = first.reshape(chans, parts * SUB)
    tables["spread_chan"] = np.kron(np.ones((steps, 1)), eye)
    return {name: np.asarray(table, np.float32).astype(jnp.bfloat16) for name, table in tables.items()}


def call(kernel, out_shapes, *operands, scratch=(), far=(), limit=12, keep=True, away=False):
    near = pl.BlockSpec(memory_space=pltpu.VMEM)
    stay = pl.BlockSpec(memory_space=pltpu.HBM)
    space = lambda i: pltpu.HBM if i in far else pltpu.VMEM
    operands = [pltpu.with_memory_space_constraint(a, space(i)) for i, a in enumerate(operands)]
    hold = lambda a: pltpu.VMEM(a.shape, a.dtype) if keep else a
    return pl.pallas_call(
        kernel,
        out_shape=jax.tree.map(hold, out_shapes),
        in_specs=[stay if i in far else near for i in range(len(operands))],
        out_specs=jax.tree.map(lambda _: stay if away else near, out_shapes),
        scratch_shapes=list(scratch),
        compiler_params=pltpu.CompilerParams(vmem_limit_bytes=limit * 1024 * 1024),
    )(*operands)


def lane_blocks(values):
    return [values[:, i * LANES : (i + 1) * LANES] for i in range(values.shape[1] // LANES)]


def pack(blocks):
    return jnp.concatenate(blocks, axis=1).astype(BF)


def lane_group(shape, chans):
    return lax.broadcasted_iota(jnp.int32, shape, 1) // chans


def halves(values, chans):
    high = values.astype(BF).astype(jnp.float32)
    group = lane_group(values.shape, chans)
    return jnp.where(group == 2, high, jnp.where(group == 3, values - high, 0.0))


def diagonal(values, chans):
    row_step = lax.broadcasted_iota(jnp.int32, values.shape, 0) // chans
    return jnp.where(row_step == lane_group(values.shape, chans), values, 0.0)


def start_copies(sems, *pairs):
    copies = [pltpu.make_async_copy(src, dst, sems.at[i]) for i, (src, dst) in enumerate(pairs)]
    for copy in copies:
        copy.start()
    return copies


def columns_kernel(
    in_hbm, pre_hbm, cot_hbm, time_hbm, col_hbm, square_hbm,
    out_ref, grad_ref, square_ref,
    in_ref, pre_ref, cot_ref, time_ref, col_ref, sems, *, chans,
):
    copies = start_copies(
        sems,
        (pre_hbm, pre_ref), (cot_hbm, cot_ref), (in_hbm, in_ref), (time_hbm, time_ref), (col_hbm, col_ref),
        (square_hbm, square_ref),
    )
    rows, cols, width = in_ref.shape
    for copy in copies[:5]:
        copy.wait()
    slopes = gelu_slope(pre_ref[...].reshape(rows * cols, width).astype(jnp.float32))
    grad = (cot_ref[...].reshape(rows * cols, width).astype(jnp.float32) * slopes).astype(BF)
    grad_ref[...] = grad
    field = in_ref[...].reshape(rows * cols, width)
    times = jnp.concatenate([dot(field, time_ref[...]), dot(grad, time_ref[...])], axis=1).astype(BF)
    col = col_ref[...]
    row = lax.broadcasted_iota(jnp.int32, col.shape, 0) % rows
    across = jnp.concatenate([jnp.where(row == r, col, jnp.zeros_like(col)) for r in range(rows)], axis=1)
    waves = dot(across, times)
    half = waves.shape[0] // 2
    in_cos, in_cos2, gr_cos, gr_cos2 = lane_blocks(waves[:half])
    in_sin, in_sin2, gr_sin, gr_sin2 = lane_blocks(waves[half:])
    alone = lane_group(in_cos.shape, chans) == 0
    last = jnp.where(alone, in_cos2, 0.0)
    for place, part in enumerate((-in_sin2, gr_cos2, -gr_sin2)):
        last = last + pltpu.roll(jnp.where(alone, part, 0.0), (place + 1) * chans, 1)
    out_ref[...] = pack(
        [
            in_cos + jnp.where(alone, 0.0, in_sin2),
            jnp.where(alone, 0.0, in_cos2) - in_sin,
            gr_cos + jnp.where(alone, 0.0, gr_sin2),
            jnp.where(alone, 0.0, gr_cos2) - gr_sin,
            last,
        ]
    )
    for copy in copies[5:]:
        copy.wait()


def bypass_terms(field, grad, place, chans):
    products = lax.dot_general(
        field, grad, (((0,), (0,)), ((), ())), preferred_element_type=jnp.float32
    )
    products = diagonal(products, chans)
    partial = products[:chans]
    for step in range(1, field.shape[1] // chans):
        partial = partial + products[step * chans : (step + 1) * chans]
    folded = sum(lane_blocks(partial))
    shift = LANES // 2
    while shift >= chans:
        folded = folded + pltpu.roll(folded, shift, 1)
        shift //= 2
    return dot(place, halves(folded, chans).astype(BF))


def mixing_kernel(
    sent_hbm, grad_hbm, long_hbm, first_hbm, bypass_ref, spread_ref, mixed_ref, long_ref, first_ref, grad_ref, sems
):
    del sent_hbm
    copies = start_copies(sems, (grad_hbm, grad_ref), (long_hbm, long_ref), (first_hbm, first_ref))
    chans = bypass_ref.shape[0]
    spread = spread_ref[...]
    across = lax.dot_general(
        bypass_ref[...], spread, (((0,), (1,)), ((), ())), preferred_element_type=jnp.float32
    ).astype(BF)
    matrix = diagonal(dot(spread, across), chans).astype(BF)
    copies[0].wait()
    mixed_ref[...] = dot(grad_ref[...], matrix)
    for copy in copies[1:]:
        copy.wait()


def quarter_turn(values, chans):
    ahead, behind = pltpu.roll(values, LANES - chans, 1), pltpu.roll(values, chans, 1)
    return jnp.where(lane_group(values.shape, chans) % 2 == 0, ahead, -behind)


def rows_kernel(in_ref, square_ref, weight_hbm, out_ref, *, chans):
    del weight_hbm
    direct = in_ref[...]
    in_re, in_im, gr_re, gr_im, last = lane_blocks(direct)
    size = square_ref.shape[1]
    turned_last = quarter_turn(last.astype(jnp.float32), chans).astype(BF)
    turned = jnp.concatenate([in_im, -in_re, gr_im, -gr_re, turned_last], axis=1)
    modes = dot(square_ref[:size], direct) + dot(square_ref[size : 2 * size], turned)
    out_ref[...] = modes.astype(BF)


def mixing_tables(table_ref):
    size = table_ref.shape[1]
    tiles = [table_ref[2 * size + i * LANES : 2 * size + (i + 1) * LANES] for i in range(3)]
    return table_ref[:size], table_ref[size : 2 * size], *tiles


def back_kernel(
    in_ref, grad_ref, weight_ref, field_ref, table_ref, sums_ref, place_ref, repeat_hbm, rows_hbm,
    out_ref, modes_ref, repeat_ref, rows_ref, sems, *, factor,
):
    chans = place_ref.shape[1]
    copies = start_copies(sems, (rows_hbm, rows_ref), (repeat_hbm, repeat_ref))
    size = table_ref.shape[1]
    order, unorder, tile_a, tile_b, tile_last = mixing_tables(table_ref)
    modes = dot(order, in_ref[...]).astype(BF)
    modes_ref[...] = modes
    steps = weight_ref.shape[2]
    wide = weight_ref.shape[4]
    lead = LANES // chans
    gr_re, gr_im, last = lane_blocks(modes_ref[...])[2:]
    first = jnp.concatenate([gr_re, gr_im], axis=1)
    blank = jnp.zeros((LANES, LANES), BF)
    tiles = [
        jnp.concatenate([jnp.concatenate([t, blank], axis=1), jnp.concatenate([blank, t], axis=1)], axis=0)
        for t in lane_blocks(tile_a) + lane_blocks(tile_b)
    ]
    group = lane_group((size, LANES), chans)
    re_sum = im_sum = jnp.zeros((size, LANES), jnp.float32)
    for k in range(steps):
        g_re, g_im = lane_blocks((dot(first, tiles[k]) if k < lead else dot(last, tile_last)).astype(BF))
        p_re, p_im = [], []
        for j in range(wide // LANES):
            w_re = weight_ref[0, :, k, :, j * LANES : (j + 1) * LANES].reshape(size, LANES)
            w_im = weight_ref[1, :, k, :, j * LANES : (j + 1) * LANES].reshape(size, LANES)
            p_re.append(w_re * g_re + w_im * g_im)
            p_im.append(w_re * g_im - w_im * g_re)
        both = jnp.concatenate([jnp.concatenate(p_re, axis=1), jnp.concatenate(p_im, axis=1)], axis=0)
        summed = dot(both, sums_ref[...])
        if k < lead:
            re_sum = jnp.where(group == k, summed[:size], re_sum)
            im_sum = jnp.where(group == k, summed[size:], im_sum)
        else:
            last_sum = jnp.where(group == 0, summed[:size], jnp.where(group == 1, summed[size:], 0.0))
    rows, cols, width = field_ref.shape
    terms = bypass_terms(field_ref[...].reshape(rows * cols, width), grad_ref[...], place_ref[...], chans)
    back = (jnp.concatenate([re_sum, im_sum, last_sum], axis=1) * factor).astype(BF)
    re, im, last = lane_blocks(dot(unorder, back))
    out_ref[...] = pack([re, im, last + terms])
    for copy in copies:
        copy.wait()


def weight_kernel(modes_ref, repeat_ref, table_ref, out_hbm, out_ref, sems, *, factor):
    slots, _, kept, count, wide = out_ref.shape
    steps = out_hbm.shape[2]
    lead = repeat_ref.shape[0] - 2
    in_re, in_im, gr_re, gr_im, last = lane_blocks(modes_ref[...])
    _, _, tile_a, tile_b, tile_last = mixing_tables(table_ref)
    tiled = [lane_blocks(dot(g, tile_a) * factor) + lane_blocks(dot(g, tile_b) * factor) for g in (gr_re, gr_im)]
    tiled = list(zip(*tiled)) + [lane_blocks(dot(last, tile_last) * factor)]
    copies = []
    for k in range(steps):
        if k < lead:
            a_re, a_im = dot(in_re, repeat_ref[k]), dot(in_im, repeat_ref[k])
        else:
            a_re, a_im = dot(last, repeat_ref[lead]), dot(last, repeat_ref[lead + 1])
        b_re, b_im = tiled[k]
        slot = k % slots
        if k >= slots:
            copies[k - slots].wait()
        for j in range(wide // LANES):
            part = slice(j * LANES, (j + 1) * LANES)
            out_ref[slot, 0, :, :, part] = (a_re[:, part] * b_re + a_im[:, part] * b_im).reshape(kept, count, LANES)
            out_ref[slot, 1, :, :, part] = (a_re[:, part] * b_im - a_im[:, part] * b_re).reshape(kept, count, LANES)
        copies.append(pltpu.make_async_copy(out_ref.at[slot], out_hbm.at[:, :, k], sems.at[slot]))
        copies[k].start()
    for copy in copies[max(0, steps - slots) :]:
        copy.wait()


def rows_back_kernel(in_ref, table_ref, out_hbm, out_ref, sems, *, chans):
    re, im, tail = lane_blocks(in_ref[...])
    size = table_ref.shape[1]
    back_cos, back_sin, total = [table_ref[i * size : (i + 1) * size] for i in range(3)]
    group = lane_group(tail.shape, chans)
    last = jnp.where(group < 2, tail.astype(jnp.float32), 0.0)
    turned_last = -quarter_turn(last, chans).astype(BF)
    last = last.astype(BF)
    direct = jnp.concatenate([re, im, last], axis=1)
    turned = jnp.concatenate([-im, re, turned_last], axis=1)
    summed = dot(total, tail)
    summed = summed + pltpu.roll(summed, LANES - chans, 1)
    summed = jnp.where(group == 2, summed, 0.0)
    terms = halves(summed + pltpu.roll(summed, chans, 1), chans)
    copies = []
    pieces = sems.shape[0]
    step, long = size // pieces, out_ref.shape[0] // pieces
    for i in range(pieces):
        here, there = slice(i * step, (i + 1) * step), slice(i * long, (i + 1) * long)
        rows = dot(back_cos[here], direct) + dot(back_sin[here], turned)
        re, im, last = lane_blocks(rows)
        out_ref[there] = pack([re, im, last + terms[here]])
        copies.append(pltpu.make_async_copy(out_ref.at[there], out_hbm.at[there], sems.at[i]))
        copies[i].start()
    for copy in copies:
        copy.wait()


def columns_back_kernel(
    in_ref, mixed_ref, first_ref, long_ref, out_hbm, bypass_hbm, out_ref, bypass_ref, sems, *, factor
):
    rows, cols, width = out_ref.shape
    chans = bypass_ref.shape[0]
    lanes = in_ref[...]
    height = lanes.shape[1]
    steps = dot(lanes, long_ref[:height]).astype(BF)
    sums = dot(first_ref[...], lane_blocks(lanes)[2])
    sums = pltpu.roll(sums + pltpu.roll(sums, LANES - chans, 1), LANES // 2, 1)
    bypass_ref[...] = sums[:, :chans] * factor
    copies = start_copies(sems, (bypass_ref, bypass_hbm))
    stacked = jnp.concatenate([steps[:, :width], steps[:, width:]], axis=0)
    pieces = sems.shape[0] - 1
    size = rows // pieces
    for i in range(pieces):
        here, part = slice(i * size, (i + 1) * size), slice(i * size * cols, (i + 1) * size * cols)
        turns = long_ref[height + i * size * cols : height + (i + 1) * size * cols]
        out_ref[here] = (dot(turns, stacked) + mixed_ref[part]).reshape(size, cols, width).astype(BF)
        copies.append(pltpu.make_async_copy(out_ref.at[here], out_hbm.at[here], sems.at[1 + i]))
        copies[-1].start()
    for copy in copies:
        copy.wait()


def local(inputs, preactivation, cotangent, spectral, bypass):
    rows, cols, width = inputs.shape
    chans = bypass.shape[0]
    steps = width // chans
    kept, col_modes, time_modes, wide = spectral.shape[1:]
    parts = lax.axis_size("row")
    pair = col_modes // parts
    fits = (
        lax.axis_size("col") == 1
        and col_modes % parts == 0
        and pair * rows == SUB
        and pair * kept == SUB
        and parts == chans
        and 4 * chans == LANES
        and time_modes == 5
        and steps == 8
        and cols % LANES == 0
    )
    if not fits:
        return general_local(inputs, preactivation, cotangent, spectral, bypass)
    row_modes = kept * parts
    total_x = rows * parts
    factor = 1.0 / math.sqrt(float(total_x * cols * steps * row_modes * col_modes * time_modes))
    bypass_factor = 1.0 / math.sqrt(float(total_x * cols * steps))
    tables = build_tables(parts, rows, cols, steps, chans, row_modes, pair, kept, col_modes, time_modes)
    stack_all = lambda arrays: jnp.asarray(np.concatenate(arrays, axis=0))
    stack = lambda *names: stack_all([tables[name] for name in names])
    square = stack("row_cos", "row_sin")
    mixing = stack_all(
        [tables["order"], tables["unorder"]] + np.split(tables["tile"], 2, axis=1) + [tables["tile_last"]]
    )
    back_table = stack("back_cos", "back_sin", "total")
    long = stack("time_back", "col_back")
    time_table, col_table, repeat, sums, spread, place, first = [
        jnp.asarray(tables[name])
        for name in ("time", "col", "repeat", "sums", "spread_chan", "place", "first")
    ]

    def swap_parts(array):
        return lax.all_to_all(array, "row", 0, 0, tiled=True)

    like = lambda array: jax.ShapeDtypeStruct(array.shape, array.dtype)
    shape = jax.ShapeDtypeStruct
    chunk = parts * SUB
    field = (rows * cols, width)
    sent, pre_grad, square = call(
        lambda *refs: columns_kernel(*refs, chans=chans),
        (shape((chunk, 5 * LANES), BF), shape(field, BF))
        + (like(square),),
        inputs, preactivation, cotangent, time_table, col_table, square,
        far=range(6),
        scratch=[pltpu.VMEM(a.shape, a.dtype) for a in (inputs, inputs, inputs, time_table, col_table)]
        + [pltpu.SemaphoreType.DMA((6,))],
    )
    weight = spectral.transpose(0, 1, 3, 2, 4)
    sent = call(
        lambda *refs: rows_kernel(*refs, chans=chans),
        shape((chunk, 5 * LANES), BF),
        swap_parts(sent), square, weight,
        far=(2,),
    )
    sent, modes, repeat, back_table = call(
        lambda *refs: back_kernel(*refs, factor=factor),
        (shape((chunk, 3 * LANES), BF), shape((kept * col_modes, 5 * LANES), BF), like(repeat), like(back_table)),
        swap_parts(sent), pre_grad, weight, inputs, mixing, sums, place, repeat, back_table,
        far=(7, 8),
        scratch=[pltpu.SemaphoreType.DMA((2,))],
    )
    near = pl.BlockSpec(memory_space=pltpu.VMEM)
    slots = 3
    grad_spectral = pl.pallas_call(
        lambda *refs: weight_kernel(*refs, factor=factor),
        out_shape=shape((2, kept, time_modes, col_modes, wide), jnp.float32),
        in_specs=[near, near, near],
        out_specs=pl.BlockSpec(memory_space=pltpu.HBM),
        scratch_shapes=[
            pltpu.VMEM((slots, 2, kept, col_modes, wide), jnp.float32), pltpu.SemaphoreType.DMA((slots,)),
        ],
        compiler_params=pltpu.CompilerParams(vmem_limit_bytes=16 * 1024 * 1024),
    )(*[pltpu.with_memory_space_constraint(a, pltpu.VMEM) for a in (modes, repeat, mixing)]).transpose(0, 1, 3, 2, 4)
    sent = call(
        lambda *refs: rows_back_kernel(*refs, chans=chans),
        shape((chunk, 3 * LANES), BF),
        swap_parts(sent), back_table,
        keep=False,
        away=True,
        scratch=[pltpu.VMEM((chunk, 3 * LANES), BF), pltpu.SemaphoreType.DMA((2,))],
    )
    mixed, long, first = call(
        mixing_kernel,
        (shape(field, jnp.float32), like(long), like(first)),
        sent, pre_grad, long, first, bypass, spread,
        far=(0, 1, 2, 3),
        scratch=[pltpu.VMEM(field, BF), pltpu.SemaphoreType.DMA((3,))],
    )
    grad_inputs, grad_bypass = call(
        lambda *refs: columns_back_kernel(*refs, factor=bypass_factor),
        (shape((rows, cols, width), BF), shape((chans, chans), jnp.float32)),
        swap_parts(sent), mixed, first, long,
        keep=False,
        away=True,
        scratch=[
            pltpu.VMEM((rows, cols, width), BF),
            pltpu.VMEM((chans, chans), jnp.float32),
            pltpu.SemaphoreType.DMA((3,)),
        ],
    )
    return (grad_inputs, grad_spectral, grad_bypass)


def solution(mesh):
    return jax.shard_map(
        local,
        mesh=mesh,
        in_specs=(
            P("row", "col", None),
            P("row", "col", None),
            P("row", "col", None),
            P(None, "row", "col", None, None),
            P(),
        ),
        out_specs=(P("row", "col", None), P(None, "row", "col", None, None), P()),
        check_vma=False,
    )
```

```python
import math

import jax
import jax.numpy as jnp
import numpy as np
from jax import lax
from jax.experimental import pallas as pl
from jax.experimental.pallas import tpu as pltpu
from jax.sharding import PartitionSpec as P

exact_mode = lax.Precision.HIGHEST


def counting(length):
    return jnp.arange(length, dtype=jnp.int32)


def kept_freq(slot_index, keep_count):
    return jnp.where(slot_index < keep_count // 2, slot_index, slot_index - keep_count)


def phase_table(outer_index, inner_index, length, direction):
    turn_count = jnp.mod(outer_index[:, None] * inner_index[None, :], length)
    angles = turn_count.astype(jnp.float32) * (2.0 * math.pi / length)
    cosine = jnp.cos(angles)
    sine_part = direction * jnp.sin(angles)
    top_rows = jnp.stack([cosine, -sine_part], axis=1)
    low_rows = jnp.stack([sine_part, cosine], axis=1)
    return jnp.stack([top_rows, low_rows], axis=0)


def time_forward(step_count, time_modes):
    turn_count = jnp.mod(counting(step_count)[:, None] * counting(time_modes)[None, :], step_count)
    angles = turn_count.astype(jnp.float32) * (2.0 * math.pi / step_count)
    return jnp.stack([jnp.cos(angles), -jnp.sin(angles)], axis=1)


def time_inverse(step_count, time_modes):
    turn_count = jnp.mod(counting(time_modes)[:, None] * counting(step_count)[None, :], step_count)
    angles = turn_count.astype(jnp.float32) * (2.0 * math.pi / step_count)
    return jnp.stack([jnp.cos(angles), -jnp.sin(angles)], axis=0)


def gelu_slope(values):
    normal_cdf = 0.5 * (1.0 + lax.erf(values * (1.0 / math.sqrt(2.0))))
    density = jnp.exp(-0.5 * values * values) * (1.0 / math.sqrt(2.0 * math.pi))
    return normal_cdf + values * density


def mix_modes(modes_in, modes_grad, weight, factor):
    in_real = modes_in[:, 0]
    in_imag = modes_in[:, 1]
    grad_real = modes_grad[:, 0]
    grad_imag = modes_grad[:, 1]
    real_part = factor * (
        in_real[..., :, None] * grad_real[..., None, :]
        + in_imag[..., :, None] * grad_imag[..., None, :]
    )
    imag_part = factor * (
        in_real[..., :, None] * grad_imag[..., None, :]
        - in_imag[..., :, None] * grad_real[..., None, :]
    )
    weight_grad = jnp.stack([real_part, imag_part], axis=0)
    w_real = weight[0]
    w_imag = weight[1]
    back_real = factor * (
        jnp.einsum("kyscd,kysd->kysc", w_real, grad_real, precision=exact_mode)
        + jnp.einsum("kyscd,kysd->kysc", w_imag, grad_imag, precision=exact_mode)
    )
    back_imag = factor * (
        jnp.einsum("kyscd,kysd->kysc", w_real, grad_imag, precision=exact_mode)
        - jnp.einsum("kyscd,kysd->kysc", w_imag, grad_real, precision=exact_mode)
    )
    return (weight_grad, jnp.stack([back_real, back_imag], axis=1))


def general_local(inputs, preactivation, cotangent, spectral, bypass):
    row_count, col_count, packed = inputs.shape
    chan_count = bypass.shape[0]
    step_count = packed // chan_count
    time_modes = spectral.shape[3]
    owned_row_modes = spectral.shape[1]
    owned_col_modes = spectral.shape[2]
    row_parts = lax.axis_size("row")
    col_parts = lax.axis_size("col")
    row_modes = owned_row_modes * row_parts
    col_modes = owned_col_modes * col_parts
    total_x = row_count * row_parts
    total_y = col_count * col_parts
    factor = 1.0 / math.sqrt(
        float(total_x * total_y * step_count * row_modes * col_modes * time_modes)
    )
    row_start = lax.axis_index("row") * row_count
    col_start = lax.axis_index("col") * col_count
    mode_width = owned_col_modes * time_modes * chan_count
    slopes = gelu_slope(preactivation.astype(jnp.float32))
    pre_grad = (cotangent.astype(jnp.float32) * slopes).astype(jnp.bfloat16)
    flat_inputs = inputs.reshape(-1, chan_count)
    flat_grad = pre_grad.reshape(-1, chan_count)
    local_bypass = jnp.einsum(
        "nc,nd->cd", flat_inputs, flat_grad, preferred_element_type=jnp.float32
    )
    bypass_total = lax.psum(local_bypass, ("row", "col"))
    grad_bypass = bypass_total * (1.0 / math.sqrt(float(total_x * total_y * step_count)))
    forward_t = time_forward(step_count, time_modes)
    col_table = phase_table(counting(col_modes), col_start + counting(col_count), total_y, -1.0)

    def column_terms(field):
        cube_view = field.astype(jnp.float32).reshape(row_count, col_count, step_count, chan_count)
        in_time = jnp.einsum("rytc,tqs->ryqsc", cube_view, forward_t, precision=exact_mode)
        return jnp.einsum("akpy,rypsc->raksc", col_table, in_time, precision=exact_mode)

    col_in, col_grad = (
        lax.psum_scatter(
            column_terms(inputs).astype(jnp.bfloat16), "col", scatter_dimension=2, tiled=True
        ).astype(jnp.float32),
        lax.psum_scatter(
            column_terms(pre_grad).astype(jnp.bfloat16), "col", scatter_dimension=2, tiled=True
        ).astype(jnp.float32),
    )
    flat_in = col_in.reshape(row_count, 2, mode_width)
    flat_cols = col_grad.reshape(row_count, 2, mode_width)
    stacked = jnp.stack([flat_in, flat_cols], axis=2)
    frequencies = kept_freq(counting(owned_row_modes * lax.axis_size("row")), row_modes)
    phases = phase_table(frequencies, row_start + counting(row_count), total_x, -1.0)
    owned_modes = lax.psum_scatter(
        jnp.einsum("akpr,rpbm->kabm", phases, stacked, precision=exact_mode),
        "row",
        scatter_dimension=0,
        tiled=True,
    )
    modes_in = owned_modes[:, :, 0]
    modes_grad = owned_modes[:, :, 1]
    mode_shape = (owned_row_modes, 2, owned_col_modes, time_modes, chan_count)
    weight = spectral.astype(jnp.float32).reshape(
        2, owned_row_modes, owned_col_modes, time_modes, chan_count, chan_count
    )
    weight_grad, back_modes = mix_modes(
        modes_in.reshape(mode_shape), modes_grad.reshape(mode_shape), weight, factor
    )
    grad_spectral = weight_grad.reshape(spectral.shape)
    flat_back = back_modes.reshape(owned_row_modes, 2, mode_width)
    mode_piece = lax.all_gather(flat_back, "row", axis=0, tiled=True)
    span_count = mode_piece.shape[0]
    frequencies = kept_freq(counting(span_count), row_modes)
    phases = phase_table(row_start + counting(row_count), frequencies, total_x, 1.0)
    rows_back = jnp.einsum("axpk,kpm->xam", phases, mode_piece, precision=exact_mode)
    rows_view = rows_back.reshape(row_count, 2, owned_col_modes, time_modes, chan_count)
    col_piece = lax.all_gather(rows_view.astype(jnp.bfloat16), "col", axis=2, tiled=True).astype(
        jnp.float32
    )
    span_count = col_piece.shape[2]
    phases = phase_table(col_start + counting(col_count), counting(span_count), total_y, 1.0)
    cells_y = jnp.zeros(
        (row_count, col_count, 2, time_modes, chan_count), jnp.float32
    ) + jnp.einsum("aypk,rpksc->ryasc", phases, col_piece, precision=exact_mode)
    kernel_grad = jnp.einsum(
        "ryasc,ast->rytc", cells_y, time_inverse(step_count, time_modes), precision=exact_mode
    )
    bypass_grad = jnp.einsum("nd,cd->nc", flat_grad, bypass, preferred_element_type=jnp.float32)
    total_grad = kernel_grad.reshape(-1, chan_count) + bypass_grad
    grad_inputs = total_grad.reshape(inputs.shape).astype(jnp.bfloat16)
    return (grad_inputs, grad_spectral, grad_bypass)


BF = jnp.bfloat16
LANES = 128
SUB = 8


def dot(a, b):
    return jnp.dot(a, b, preferred_element_type=jnp.float32)


def cos_sin(turns, length):
    angles = 2.0 * np.pi * np.mod(turns, length) / length
    return np.cos(angles), np.sin(angles)


def build_tables(parts, rows, cols, steps, chans, row_modes, pair, kept, col_modes, time_modes):
    lead = LANES // chans
    eye = np.eye(chans)
    t_index = np.arange(steps)
    tables = {}
    cos_t, sin_t = cos_sin(np.outer(t_index, np.arange(time_modes)), steps)
    real = [np.kron(cos_t[:, k : k + 1], eye) for k in range(time_modes)]
    imag = [np.kron(-sin_t[:, k : k + 1], eye) for k in range(1, lead)]
    tables["time"] = np.concatenate(real + imag, axis=1)
    ky = np.arange(col_modes)
    y = np.arange(cols)
    cos_y, sin_y = cos_sin(np.outer(ky, y), cols)
    tables["col"] = np.repeat(np.concatenate([cos_y, sin_y], axis=0), rows, axis=0)
    same_row = np.eye(rows)
    col_cos = np.einsum("ky,rs->krsy", cos_y, same_row).reshape(col_modes * rows, rows * cols)
    col_sin = np.einsum("ky,rs->krsy", sin_y, same_row).reshape(col_modes * rows, rows * cols)
    slot = np.arange(row_modes)
    freq = np.where(slot < row_modes // 2, slot, slot - row_modes)
    total_x = parts * rows
    cos_x, sin_x = cos_sin(np.outer(freq, np.arange(total_x)), total_x)
    same_pair = np.eye(pair)

    def spread(matrix):
        blocks = matrix.reshape(parts, kept, parts, rows)
        return np.einsum("ekdr,pq->epkdqr", blocks, same_pair).reshape(
            parts * pair * kept, parts * pair * rows
        )

    tables["row_cos"] = spread(cos_x)
    tables["row_sin"] = spread(sin_x)
    tables["back_cos"] = spread(cos_x).T
    tables["back_sin"] = spread(sin_x).T
    order = np.zeros((kept, col_modes, parts, pair, kept))
    for k in range(kept):
        for e in range(parts):
            for p in range(pair):
                order[k, e * pair + p, e, p, k] = 1.0
    tables["order"] = order.reshape(kept * col_modes, parts * pair * kept)
    tables["unorder"] = tables["order"].T
    wide = chans * chans
    repeat = np.kron(eye, np.ones((1, chans)))
    tiled = np.kron(np.ones((1, lead)), eye)
    group = np.zeros((lead + 1, LANES, wide))
    for k in range(lead):
        group[k, k * chans : (k + 1) * chans] = repeat
    extra = np.zeros((LANES, wide))
    extra[chans : 2 * chans] = repeat
    group[lead, :chans] = repeat
    tables["repeat"] = np.concatenate([group, extra[None]], axis=0)
    spots = np.eye(lead)
    tables["tile"] = np.concatenate([np.kron(spots[:, k : k + 1], tiled) for k in range(lead)], axis=1)
    tables["tile_last"] = np.concatenate([np.kron(spots[:, k : k + 1], tiled) for k in (2, 3)], axis=1)
    tables["sums"] = np.tile(repeat.T, (1, lead))
    re_c, re_s = np.kron(cos_t.T, eye), np.kron(sin_t.T, eye)
    cut = lead * chans
    rest = np.zeros((LANES - 2 * chans, steps * chans))
    to_cos = np.concatenate([re_c[:cut], -re_s[:cut], re_c[cut:], -re_s[cut:], rest], axis=0)
    to_sin = np.concatenate([-re_s[:cut], -re_c[:cut], -re_s[cut:], -re_c[cut:], rest], axis=0)
    tables["time_back"] = np.concatenate([to_cos, to_sin], axis=1)
    tables["col_back"] = np.concatenate([col_cos.T, col_sin.T], axis=1)
    place = np.zeros((parts, SUB, chans))
    for c in range(chans):
        place[c, :, c] = 1.0
    tables["place"] = place.reshape(parts * SUB, chans)
    pick = np.zeros((parts, SUB))
    pick[:, 0] = 1.0
    tables["total"] = np.broadcast_to(pick.reshape(1, -1), (parts * SUB, parts * SUB))
    first = np.zeros((chans, parts, SUB))
    for c in range(chans):
        first[c, c, 0] = 1.0
    tables["first"] = first.reshape(chans, parts * SUB)
    tables["spread_chan"] = np.kron(np.ones((steps, 1)), eye)
    return {name: np.asarray(table, np.float32).astype(jnp.bfloat16) for name, table in tables.items()}


def call(kernel, out_shapes, *operands, scratch=(), far=(), limit=12, keep=True, away=False):
    near = pl.BlockSpec(memory_space=pltpu.VMEM)
    stay = pl.BlockSpec(memory_space=pltpu.HBM)
    space = lambda i: pltpu.HBM if i in far else pltpu.VMEM
    operands = [pltpu.with_memory_space_constraint(a, space(i)) for i, a in enumerate(operands)]
    hold = lambda a: pltpu.VMEM(a.shape, a.dtype) if keep else a
    return pl.pallas_call(
        kernel,
        out_shape=jax.tree.map(hold, out_shapes),
        in_specs=[stay if i in far else near for i in range(len(operands))],
        out_specs=jax.tree.map(lambda _: stay if away else near, out_shapes),
        scratch_shapes=list(scratch),
        compiler_params=pltpu.CompilerParams(vmem_limit_bytes=limit * 1024 * 1024),
    )(*operands)


def lane_blocks(values):
    return [values[:, i * LANES : (i + 1) * LANES] for i in range(values.shape[1] // LANES)]


def pack(blocks):
    return jnp.concatenate(blocks, axis=1).astype(BF)


def lane_group(shape, chans):
    return lax.broadcasted_iota(jnp.int32, shape, 1) // chans


def halves(values, chans):
    high = values.astype(BF).astype(jnp.float32)
    group = lane_group(values.shape, chans)
    return jnp.where(group == 2, high, jnp.where(group == 3, values - high, 0.0))


def diagonal(values, chans):
    row_step = lax.broadcasted_iota(jnp.int32, values.shape, 0) // chans
    return jnp.where(row_step == lane_group(values.shape, chans), values, 0.0)


def start_copies(sems, *pairs):
    copies = [pltpu.make_async_copy(src, dst, sems.at[i]) for i, (src, dst) in enumerate(pairs)]
    for copy in copies:
        copy.start()
    return copies


def columns_kernel(
    in_hbm, pre_hbm, cot_hbm, time_hbm, col_hbm, square_hbm,
    out_ref, grad_ref, square_ref,
    in_ref, pre_ref, cot_ref, time_ref, col_ref, sems, *, chans,
):
    copies = start_copies(
        sems,
        (pre_hbm, pre_ref), (cot_hbm, cot_ref), (in_hbm, in_ref), (time_hbm, time_ref), (col_hbm, col_ref),
        (square_hbm, square_ref),
    )
    rows, cols, width = in_ref.shape
    for copy in copies[:5]:
        copy.wait()
    slopes = gelu_slope(pre_ref[...].reshape(rows * cols, width).astype(jnp.float32))
    grad = (cot_ref[...].reshape(rows * cols, width).astype(jnp.float32) * slopes).astype(BF)
    grad_ref[...] = grad
    field = in_ref[...].reshape(rows * cols, width)
    times = jnp.concatenate([dot(field, time_ref[...]), dot(grad, time_ref[...])], axis=1).astype(BF)
    col = col_ref[...]
    row = lax.broadcasted_iota(jnp.int32, col.shape, 0) % rows
    across = jnp.concatenate([jnp.where(row == r, col, jnp.zeros_like(col)) for r in range(rows)], axis=1)
    waves = dot(across, times)
    half = waves.shape[0] // 2
    in_cos, in_cos2, gr_cos, gr_cos2 = lane_blocks(waves[:half])
    in_sin, in_sin2, gr_sin, gr_sin2 = lane_blocks(waves[half:])
    alone = lane_group(in_cos.shape, chans) == 0
    last = jnp.where(alone, in_cos2, 0.0)
    for place, part in enumerate((-in_sin2, gr_cos2, -gr_sin2)):
        last = last + pltpu.roll(jnp.where(alone, part, 0.0), (place + 1) * chans, 1)
    out_ref[...] = pack(
        [
            in_cos + jnp.where(alone, 0.0, in_sin2),
            jnp.where(alone, 0.0, in_cos2) - in_sin,
            gr_cos + jnp.where(alone, 0.0, gr_sin2),
            jnp.where(alone, 0.0, gr_cos2) - gr_sin,
            last,
        ]
    )
    for copy in copies[5:]:
        copy.wait()


def bypass_terms(field, grad, place, chans):
    products = lax.dot_general(
        field, grad, (((0,), (0,)), ((), ())), preferred_element_type=jnp.float32
    )
    products = diagonal(products, chans)
    partial = products[:chans]
    for step in range(1, field.shape[1] // chans):
        partial = partial + products[step * chans : (step + 1) * chans]
    folded = sum(lane_blocks(partial))
    shift = LANES // 2
    while shift >= chans:
        folded = folded + pltpu.roll(folded, shift, 1)
        shift //= 2
    return dot(place, halves(folded, chans).astype(BF))


def mixing_kernel(
    sent_hbm, grad_hbm, long_hbm, first_hbm, bypass_ref, spread_ref, mixed_ref, long_ref, first_ref, grad_ref, sems
):
    del sent_hbm
    copies = start_copies(sems, (grad_hbm, grad_ref), (long_hbm, long_ref), (first_hbm, first_ref))
    chans = bypass_ref.shape[0]
    spread = spread_ref[...]
    across = lax.dot_general(
        bypass_ref[...], spread, (((0,), (1,)), ((), ())), preferred_element_type=jnp.float32
    ).astype(BF)
    matrix = diagonal(dot(spread, across), chans).astype(BF)
    copies[0].wait()
    mixed_ref[...] = dot(grad_ref[...], matrix)
    for copy in copies[1:]:
        copy.wait()


def quarter_turn(values, chans):
    ahead, behind = pltpu.roll(values, LANES - chans, 1), pltpu.roll(values, chans, 1)
    return jnp.where(lane_group(values.shape, chans) % 2 == 0, ahead, -behind)


def rows_kernel(in_ref, square_ref, weight_hbm, out_ref, *, chans):
    del weight_hbm
    direct = in_ref[...]
    in_re, in_im, gr_re, gr_im, last = lane_blocks(direct)
    size = square_ref.shape[1]
    turned_last = quarter_turn(last.astype(jnp.float32), chans).astype(BF)
    turned = jnp.concatenate([in_im, -in_re, gr_im, -gr_re, turned_last], axis=1)
    phases = jnp.concatenate([square_ref[:size], square_ref[size : 2 * size]], axis=1)
    modes = dot(phases, jnp.concatenate([direct, turned], axis=0))
    out_ref[...] = modes.astype(BF)


def mixing_tables(table_ref):
    size = table_ref.shape[1]
    tiles = [table_ref[2 * size + i * LANES : 2 * size + (i + 1) * LANES] for i in range(3)]
    return table_ref[:size], table_ref[size : 2 * size], *tiles


def back_kernel(
    in_ref, grad_ref, weight_ref, field_ref, table_ref, sums_ref, place_ref, repeat_hbm, rows_hbm,
    out_ref, modes_ref, repeat_ref, rows_ref, sems, *, factor,
):
    chans = place_ref.shape[1]
    copies = start_copies(sems, (rows_hbm, rows_ref), (repeat_hbm, repeat_ref))
    size = table_ref.shape[1]
    order, unorder, tile_a, tile_b, tile_last = mixing_tables(table_ref)
    modes = dot(order, in_ref[...]).astype(BF)
    modes_ref[...] = modes
    steps = weight_ref.shape[2]
    wide = weight_ref.shape[4]
    lead = LANES // chans
    gr_re, gr_im, last = lane_blocks(modes_ref[...])[2:]
    first = jnp.concatenate([gr_re, gr_im], axis=1)
    blank = jnp.zeros((LANES, LANES), BF)
    tiles = [
        jnp.concatenate([jnp.concatenate([t, blank], axis=1), jnp.concatenate([blank, t], axis=1)], axis=0)
        for t in lane_blocks(tile_a) + lane_blocks(tile_b)
    ]
    group = lane_group((size, LANES), chans)
    re_sum = im_sum = jnp.zeros((size, LANES), jnp.float32)
    for k in range(steps):
        g_re, g_im = lane_blocks((dot(first, tiles[k]) if k < lead else dot(last, tile_last)).astype(BF))
        p_re, p_im = [], []
        for j in range(wide // LANES):
            w_re = weight_ref[0, :, k, :, j * LANES : (j + 1) * LANES].reshape(size, LANES)
            w_im = weight_ref[1, :, k, :, j * LANES : (j + 1) * LANES].reshape(size, LANES)
            p_re.append(w_re * g_re + w_im * g_im)
            p_im.append(w_re * g_im - w_im * g_re)
        both = jnp.concatenate([jnp.concatenate(p_re, axis=1), jnp.concatenate(p_im, axis=1)], axis=0)
        summed = dot(both, sums_ref[...])
        if k < lead:
            re_sum = jnp.where(group == k, summed[:size], re_sum)
            im_sum = jnp.where(group == k, summed[size:], im_sum)
        else:
            last_sum = jnp.where(group == 0, summed[:size], jnp.where(group == 1, summed[size:], 0.0))
    rows, cols, width = field_ref.shape
    terms = bypass_terms(field_ref[...].reshape(rows * cols, width), grad_ref[...], place_ref[...], chans)
    back = (jnp.concatenate([re_sum, im_sum, last_sum], axis=1) * factor).astype(BF)
    re, im, last = lane_blocks(dot(unorder, back))
    out_ref[...] = pack([re, im, last + terms])
    for copy in copies:
        copy.wait()


def weight_kernel(modes_ref, repeat_ref, table_ref, out_hbm, out_ref, sems, *, factor):
    slots, _, kept, count, wide = out_ref.shape
    steps = out_hbm.shape[2]
    lead = repeat_ref.shape[0] - 2
    in_re, in_im, gr_re, gr_im, last = lane_blocks(modes_ref[...])
    _, _, tile_a, tile_b, tile_last = mixing_tables(table_ref)
    tiled = [lane_blocks(dot(g, tile_a) * factor) + lane_blocks(dot(g, tile_b) * factor) for g in (gr_re, gr_im)]
    tiled = list(zip(*tiled)) + [lane_blocks(dot(last, tile_last) * factor)]
    copies = []
    for k in range(steps):
        if k < lead:
            a_re, a_im = dot(in_re, repeat_ref[k]), dot(in_im, repeat_ref[k])
        else:
            a_re, a_im = dot(last, repeat_ref[lead]), dot(last, repeat_ref[lead + 1])
        b_re, b_im = tiled[k]
        slot = k % slots
        if k >= slots:
            copies[k - slots].wait()
        for j in range(wide // LANES):
            part = slice(j * LANES, (j + 1) * LANES)
            out_ref[slot, 0, :, :, part] = (a_re[:, part] * b_re + a_im[:, part] * b_im).reshape(kept, count, LANES)
            out_ref[slot, 1, :, :, part] = (a_re[:, part] * b_im - a_im[:, part] * b_re).reshape(kept, count, LANES)
        copies.append(pltpu.make_async_copy(out_ref.at[slot], out_hbm.at[:, :, k], sems.at[slot]))
        copies[k].start()
    for copy in copies[max(0, steps - slots) :]:
        copy.wait()


def rows_back_kernel(in_ref, table_ref, out_hbm, out_ref, sems, *, chans):
    re, im, tail = lane_blocks(in_ref[...])
    size = table_ref.shape[1]
    back_cos, back_sin, total = [table_ref[i * size : (i + 1) * size] for i in range(3)]
    group = lane_group(tail.shape, chans)
    last = jnp.where(group < 2, tail.astype(jnp.float32), 0.0)
    turned_last = -quarter_turn(last, chans).astype(BF)
    last = last.astype(BF)
    direct = jnp.concatenate([re, im, last], axis=1)
    turned = jnp.concatenate([-im, re, turned_last], axis=1)
    summed = dot(total, tail)
    summed = summed + pltpu.roll(summed, LANES - chans, 1)
    summed = jnp.where(group == 2, summed, 0.0)
    terms = halves(summed + pltpu.roll(summed, chans, 1), chans)
    both = jnp.concatenate([direct, turned], axis=0)
    copies = []
    pieces = sems.shape[0]
    step, long = size // pieces, out_ref.shape[0] // pieces
    for i in range(pieces):
        here, there = slice(i * step, (i + 1) * step), slice(i * long, (i + 1) * long)
        rows = dot(jnp.concatenate([back_cos[here], back_sin[here]], axis=1), both)
        re, im, last = lane_blocks(rows)
        out_ref[there] = pack([re, im, last + terms[here]])
        copies.append(pltpu.make_async_copy(out_ref.at[there], out_hbm.at[there], sems.at[i]))
        copies[i].start()
    for copy in copies:
        copy.wait()


def columns_back_kernel(
    in_ref, mixed_ref, first_ref, long_ref, out_hbm, bypass_hbm, out_ref, bypass_ref, sems, *, factor
):
    rows, cols, width = out_ref.shape
    chans = bypass_ref.shape[0]
    lanes = in_ref[...]
    height = lanes.shape[1]
    steps = dot(lanes, long_ref[:height]).astype(BF)
    sums = dot(first_ref[...], lane_blocks(lanes)[2])
    sums = pltpu.roll(sums + pltpu.roll(sums, LANES - chans, 1), LANES // 2, 1)
    bypass_ref[...] = sums[:, :chans] * factor
    copies = start_copies(sems, (bypass_ref, bypass_hbm))
    stacked = jnp.concatenate([steps[:, :width], steps[:, width:]], axis=0)
    pieces = sems.shape[0] - 1
    size = rows // pieces
    for i in range(pieces):
        here, part = slice(i * size, (i + 1) * size), slice(i * size * cols, (i + 1) * size * cols)
        turns = long_ref[height + i * size * cols : height + (i + 1) * size * cols]
        out_ref[here] = (dot(turns, stacked) + mixed_ref[part]).reshape(size, cols, width).astype(BF)
        copies.append(pltpu.make_async_copy(out_ref.at[here], out_hbm.at[here], sems.at[1 + i]))
        copies[-1].start()
    for copy in copies:
        copy.wait()


def local(inputs, preactivation, cotangent, spectral, bypass):
    rows, cols, width = inputs.shape
    chans = bypass.shape[0]
    steps = width // chans
    kept, col_modes, time_modes, wide = spectral.shape[1:]
    parts = lax.axis_size("row")
    pair = col_modes // parts
    fits = (
        lax.axis_size("col") == 1
        and col_modes % parts == 0
        and pair * rows == SUB
        and pair * kept == SUB
        and parts == chans
        and 4 * chans == LANES
        and time_modes == 5
        and steps == 8
        and cols % LANES == 0
    )
    if not fits:
        return general_local(inputs, preactivation, cotangent, spectral, bypass)
    row_modes = kept * parts
    total_x = rows * parts
    factor = 1.0 / math.sqrt(float(total_x * cols * steps * row_modes * col_modes * time_modes))
    bypass_factor = 1.0 / math.sqrt(float(total_x * cols * steps))
    tables = build_tables(parts, rows, cols, steps, chans, row_modes, pair, kept, col_modes, time_modes)
    stack_all = lambda arrays: jnp.asarray(np.concatenate(arrays, axis=0))
    stack = lambda *names: stack_all([tables[name] for name in names])
    square = stack("row_cos", "row_sin")
    mixing = stack_all(
        [tables["order"], tables["unorder"]] + np.split(tables["tile"], 2, axis=1) + [tables["tile_last"]]
    )
    back_table = stack("back_cos", "back_sin", "total")
    long = stack("time_back", "col_back")
    time_table, col_table, repeat, sums, spread, place, first = [
        jnp.asarray(tables[name])
        for name in ("time", "col", "repeat", "sums", "spread_chan", "place", "first")
    ]

    def swap_parts(array):
        return lax.all_to_all(array, "row", 0, 0, tiled=True)

    like = lambda array: jax.ShapeDtypeStruct(array.shape, array.dtype)
    shape = jax.ShapeDtypeStruct
    chunk = parts * SUB
    field = (rows * cols, width)
    sent, pre_grad, square = call(
        lambda *refs: columns_kernel(*refs, chans=chans),
        (shape((chunk, 5 * LANES), BF), shape(field, BF))
        + (like(square),),
        inputs, preactivation, cotangent, time_table, col_table, square,
        far=range(6),
        scratch=[pltpu.VMEM(a.shape, a.dtype) for a in (inputs, inputs, inputs, time_table, col_table)]
        + [pltpu.SemaphoreType.DMA((6,))],
    )
    weight = spectral.transpose(0, 1, 3, 2, 4)
    sent = call(
        lambda *refs: rows_kernel(*refs, chans=chans),
        shape((chunk, 5 * LANES), BF),
        swap_parts(sent), square, weight,
        far=(2,),
    )
    sent, modes, repeat, back_table = call(
        lambda *refs: back_kernel(*refs, factor=factor),
        (shape((chunk, 3 * LANES), BF), shape((kept * col_modes, 5 * LANES), BF), like(repeat), like(back_table)),
        swap_parts(sent), pre_grad, weight, inputs, mixing, sums, place, repeat, back_table,
        far=(7, 8),
        scratch=[pltpu.SemaphoreType.DMA((2,))],
    )
    near = pl.BlockSpec(memory_space=pltpu.VMEM)
    slots = 3
    grad_spectral = pl.pallas_call(
        lambda *refs: weight_kernel(*refs, factor=factor),
        out_shape=shape((2, kept, time_modes, col_modes, wide), jnp.float32),
        in_specs=[near, near, near],
        out_specs=pl.BlockSpec(memory_space=pltpu.HBM),
        scratch_shapes=[
            pltpu.VMEM((slots, 2, kept, col_modes, wide), jnp.float32), pltpu.SemaphoreType.DMA((slots,)),
        ],
        compiler_params=pltpu.CompilerParams(vmem_limit_bytes=16 * 1024 * 1024),
    )(*[pltpu.with_memory_space_constraint(a, pltpu.VMEM) for a in (modes, repeat, mixing)]).transpose(0, 1, 3, 2, 4)
    sent = call(
        lambda *refs: rows_back_kernel(*refs, chans=chans),
        shape((chunk, 3 * LANES), BF),
        swap_parts(sent), back_table,
        keep=False,
        away=True,
        scratch=[pltpu.VMEM((chunk, 3 * LANES), BF), pltpu.SemaphoreType.DMA((2,))],
    )
    mixed, long, first = call(
        mixing_kernel,
        (shape(field, jnp.float32), like(long), like(first)),
        sent, pre_grad, long, first, bypass, spread,
        far=(0, 1, 2, 3),
        scratch=[pltpu.VMEM(field, BF), pltpu.SemaphoreType.DMA((3,))],
    )
    grad_inputs, grad_bypass = call(
        lambda *refs: columns_back_kernel(*refs, factor=bypass_factor),
        (shape((rows, cols, width), BF), shape((chans, chans), jnp.float32)),
        swap_parts(sent), mixed, first, long,
        keep=False,
        away=True,
        scratch=[
            pltpu.VMEM((rows, cols, width), BF),
            pltpu.VMEM((chans, chans), jnp.float32),
            pltpu.SemaphoreType.DMA((3,)),
        ],
    )
    return (grad_inputs, grad_spectral, grad_bypass)


def solution(mesh):
    return jax.shard_map(
        local,
        mesh=mesh,
        in_specs=(
            P("row", "col", None),
            P("row", "col", None),
            P("row", "col", None),
            P(None, "row", "col", None, None),
            P(),
        ),
        out_specs=(P("row", "col", None), P(None, "row", "col", None, None), P()),
        check_vma=False,
    )
```
